32 devices in a mesh: dp: 4 (over y, x), expert: 8 (over z, core).
Axes of the slice: x: 2, y: 2, z: 4, core: 2. Of those that a mesh axis runs over, the one named last changes fastest.
Arguments:
- tokens: bfloat16 [8192, 2048], P(('dp', 'expert')), may hold values from -6 to 6
- out_grad: bfloat16 [8192, 2048], P(('dp', 'expert')), may hold values from -6 to 6
- token_picks: int32 [32, 16, 8], P(('dp', 'expert')), may hold values from 0 to 255, as said below
- router: bfloat16 [2048, 16], P(None, 'expert'), may hold values from -0.125 to 0.125
- kept_blocks: int32 [16, 3, 128], P('expert'), may hold values from 0 to 384, as said below
- masters: float32 [16, 3, 128, 4096], P('expert', None, 'dp'), may hold values from -0.25 to 0.25
- scores: float32 [16, 3, 128], P('expert', None, 'dp'), may hold values from -6 to 6
Outputs:
- layer_out: bfloat16 [8192, 2048], P(('dp', 'expert'))
- input_grad: bfloat16 [8192, 2048], P(('dp', 'expert'))
- master_new: float32 [16, 3, 128, 4096], P('expert', None, 'dp')
- score_new: float32 [16, 3, 128], P('expert', None, 'dp')
- router_grad: float32 [2048, 16], P('dp', 'expert')
The draws below stay inside these ranges and needn't reach their ends.
Inputs may be any that keep to these rules, and one draw needn't show every extreme that they name: `token_picks`: within one source block and one expert the 8 picks are distinct tokens. `kept_blocks`: each list of 128 slots holds, in ascending order, between 64 and 128 distinct block numbers below 384, then 384 in the remaining slots; for each of the three matrices the list of some expert is full.
All inputs are finite; a program needn't handle non-finite values.
Results may differ from the reference program's by a relative error of at most 0.0081.
Values may be sent and summed in bfloat16 or wider, within the bound.
A program may use at most 192 MiB of HBM per device.

```python
import jax
import jax.numpy as jnp
from jax import lax

D = 2048
FF = 768
BS = 64
MAXB = 128
TOK_DEV = 256
CAP = 8
E = 16
GROUP = 8
SOURCES = 32
TOKENS = 8192
N_DP = 4


def draw_token_picks(key, part):
    keys = jax.random.split(jax.random.fold_in(key, 11), SOURCES * E)
    chosen = jax.vmap(lambda single: jax.random.permutation(single, TOK_DEV)[:CAP])(keys)
    return chosen.reshape(SOURCES, E, CAP).astype(jnp.int32)


def draw_kept_blocks(key, part):
    blocks_total = D // BS * (FF // BS)
    count_key = jax.random.fold_in(key, 21)
    full_key = jax.random.fold_in(key, 22)
    order_key = jax.random.fold_in(key, 23)
    counts = jax.random.randint(count_key, (E, 3), MAXB // 2, MAXB + 1)
    fullest = jax.random.randint(full_key, (3,), 0, E)
    counts = jnp.where(jnp.arange(E)[:, None] == fullest[None, :], MAXB, counts)
    keys = jax.random.split(order_key, E * 3)
    chosen = jax.vmap(lambda single: jax.random.permutation(single, blocks_total)[:MAXB])(keys)
    chosen = chosen.reshape(E, 3, MAXB).astype(jnp.int32)
    slots = jnp.arange(MAXB)[None, None, :]
    chosen = jnp.where(slots < counts[:, :, None], chosen, blocks_total)
    return jnp.sort(chosen, axis=-1).astype(jnp.int32)


def block_scale(rng, dims, shards, smallest, top_value):
    factor_of, own = 1.0, jax.random.fold_in(rng, 6)
    for dim, blocks in shards:
        heights = jnp.exp(jax.random.uniform(jax.random.fold_in(own, dim), (blocks,), jnp.float32, smallest / len(shards), top_value / len(shards)))
        factor_of = factor_of * jnp.repeat(heights, dims[dim] // blocks).reshape([-1 if axis == dim else 1 for axis in range(len(dims))])
    return factor_of


def gaussian(stream_key, shape, deviation, limit, cuts=(), held_as=jnp.bfloat16):
    drawn = deviation * jax.random.normal(stream_key, shape, jnp.float32)
    if cuts:
        drawn = drawn * block_scale(stream_key, shape, cuts, -0.22, 0.18)
    return jnp.clip(drawn, -limit, limit).astype(held_as)


def setup_inputs(seed: int = 0) -> dict:
    arg_keys = jax.random.split(jax.random.key(seed), 8)
    return {
        "tokens": gaussian(arg_keys[0], (TOKENS, D), 1.0, 6.0, ((0, 32),)),
        "out_grad": gaussian(arg_keys[1], (TOKENS, D), 1.0, 6.0, ((0, 32),)),
        "token_picks": draw_token_picks(jax.random.fold_in(arg_keys[7], 71), 0),
        "router": gaussian(arg_keys[3], (D, E), D ** -0.5, 0.125, ((1, 8),)),
        "kept_blocks": draw_kept_blocks(jax.random.fold_in(arg_keys[7], 71), 0),
        "masters": gaussian(arg_keys[5], (E, 3, MAXB, BS * BS), (D // 4) ** -0.5, 0.25, ((0, 8), (2, 4)), jnp.float32),
        "scores": gaussian(arg_keys[6], (E, 3, MAXB), 1.0, 6.0, ((0, 8), (2, 4)), jnp.float32),
    }


LEARN_RATE = 0.005
SCORE_RATE = 0.05

def layouts(kept_rows, in_blocks, hid_blocks):
    blocks_total = in_blocks * hid_blocks
    plan_list = []
    for matrix, col_count in ((0, hid_blocks), (1, hid_blocks), (2, in_blocks)):
        usable = kept_rows[matrix] < blocks_total
        safe_index = jnp.where(usable, kept_rows[matrix], 0).astype(jnp.int32)
        plan_list.append((safe_index // col_count, safe_index % col_count, usable, safe_index))
    return plan_list

def masked_tiles(tile_stack, plan_list):
    return [jnp.where(plan_list[matrix][2][:, None, None], tile_stack[matrix], jnp.zeros_like(tile_stack[matrix])) for matrix in range(3)]

def sparse_apply(operand, tile_set, src_blocks, dst_blocks, usable, out_blocks):
    row_count = operand.shape[0]
    tile_width = tile_set.shape[-1]
    pieces = jnp.take(operand.reshape(row_count, -1, tile_width), src_blocks, axis=1)
    partial_out = jnp.einsum('rmk,mkn->rmn', pieces.astype(jnp.float32), tile_set.astype(jnp.float32), precision=lax.Precision.HIGHEST)
    placer = ((dst_blocks[:, None] == jnp.arange(out_blocks)[None, :]) & usable[:, None]).astype(jnp.float32)
    placed = jnp.einsum('rmn,mc->rcn', partial_out, placer, precision=lax.Precision.HIGHEST)
    return placed.reshape(row_count, out_blocks * tile_width)

def project(operand, weight, flipped, row_blocks, col_blocks):
    tile_set, block_plan = weight
    if flipped:
        return sparse_apply(operand, jnp.swapaxes(tile_set, 1, 2), block_plan[1], block_plan[0], block_plan[2], row_blocks)
    return sparse_apply(operand, tile_set, block_plan[0], block_plan[1], block_plan[2], col_blocks)

def weight_grad(operand, cotangent, weight):
    tile_set, block_plan = weight
    tile_width = tile_set.shape[-1]
    row_count = operand.shape[0]
    left_part = jnp.take(operand.reshape(row_count, -1, tile_width), block_plan[0], axis=1).astype(jnp.float32)
    right_part = jnp.take(cotangent.reshape(row_count, -1, tile_width), block_plan[1], axis=1).astype(jnp.float32)
    gradient = jnp.einsum('rmk,rmn->mkn', left_part, right_part, precision=lax.Precision.HIGHEST)
    gradient = jnp.where(block_plan[2][:, None, None], gradient, jnp.zeros_like(gradient))
    return gradient.reshape(-1, tile_width * tile_width)

def expert_forward(rows_in, weights, router_col, in_blocks, hid_blocks):
    gate_pre = project(rows_in, weights[0], False, in_blocks, hid_blocks)
    up_pre = project(rows_in, weights[1], False, in_blocks, hid_blocks)
    hidden = (jax.nn.silu(gate_pre) * up_pre).astype(jnp.bfloat16)
    output = project(hidden, weights[2], False, hid_blocks, in_blocks)
    gating = jax.nn.sigmoid(jnp.dot(rows_in, router_col, preferred_element_type=jnp.float32))
    part_out = (gating[:, None] * output).astype(jnp.bfloat16)
    return (part_out, (gate_pre, up_pre, hidden, output, gating))

def expert_down_grad(grad_rows, saved_state, weights, in_blocks, hid_blocks):
    gate_pre, up_pre, hidden, output, gating = saved_state
    grad_float = grad_rows.astype(jnp.float32)
    logit_grad = lax.optimization_barrier(jnp.sum(grad_float * output, axis=1)) * gating * (1.0 - gating)
    scaled = (gating[:, None] * grad_float).astype(jnp.bfloat16)
    down_grad = weight_grad(hidden, scaled, weights[2])
    hidden_grad = project(scaled, weights[2], True, hid_blocks, in_blocks)
    return (down_grad, (hidden_grad, logit_grad))

def expert_rest_grad(rows_in, carried, saved_state, weights, router_col, in_blocks, hid_blocks):
    hidden_grad, logit_grad = carried
    gate_pre, up_pre = (saved_state[0], saved_state[1])
    sigmoid = jax.nn.sigmoid(gate_pre)
    gate_grad = (hidden_grad * up_pre * sigmoid * (1.0 + gate_pre * (1.0 - sigmoid))).astype(jnp.bfloat16)
    up_grad = (hidden_grad * gate_pre * sigmoid).astype(jnp.bfloat16)
    gate_weight = weight_grad(rows_in, gate_grad, weights[0])
    up_weight = weight_grad(rows_in, up_grad, weights[1])
    input_part = project(gate_grad, weights[0], True, in_blocks, hid_blocks) + project(up_grad, weights[1], True, in_blocks, hid_blocks)
    input_part = input_part + logit_grad[:, None] * router_col.astype(jnp.float32)[None, :]
    router_part = jnp.dot(logit_grad, rows_in.astype(jnp.float32), precision=lax.Precision.HIGHEST)
    return (input_part.astype(jnp.bfloat16), gate_weight, up_weight, router_part)

def reference(tokens, out_grad, token_picks, router, kept_blocks, masters, scores):
    in_blocks = D // BS
    hid_blocks = FF // BS
    copies = masters.astype(jnp.bfloat16).reshape(E, 3, MAXB, BS, BS)
    starts = (jnp.arange(SOURCES) * TOK_DEV).astype(jnp.int32)[:, None]
    picks_by_expert = jnp.transpose(token_picks, (1, 0, 2))

    def one_expert(carried_sums, expert_item):
        out_sum, input_sum = carried_sums
        kept_rows, tile_stack, router_col, chosen = expert_item
        plan_list = layouts(kept_rows, in_blocks, hid_blocks)
        tile_list = masked_tiles(tile_stack, plan_list)
        weights = [(tile_list[matrix], plan_list[matrix]) for matrix in range(3)]
        index_all = (chosen.astype(jnp.int32) + starts).astype(jnp.int32)
        grads = jnp.zeros((3, MAXB, BS * BS), jnp.float32)
        router_sum = jnp.zeros((D,), jnp.float32)
        for dp_group in range(N_DP):
            row_index = index_all[dp_group * GROUP:(dp_group + 1) * GROUP].reshape(-1)
            rows_in = tokens[row_index]
            grad_rows = out_grad[row_index]
            part_out, saved_state = expert_forward(rows_in, weights, router_col, in_blocks, hid_blocks)
            down_grad, inner_state = expert_down_grad(grad_rows, saved_state, weights, in_blocks, hid_blocks)
            input_part, gate_weight, up_weight, router_part = expert_rest_grad(rows_in, inner_state, saved_state, weights, router_col, in_blocks, hid_blocks)
            grads = grads + jnp.stack([gate_weight, up_weight, down_grad])
            router_sum = router_sum + router_part
            out_sum = out_sum.at[row_index].add(part_out.astype(jnp.float32))
            input_sum = input_sum.at[row_index].add(input_part.astype(jnp.float32))
        return ((out_sum, input_sum), (grads, router_sum))
    zeros_init = (jnp.zeros((TOKENS, D), jnp.float32), jnp.zeros((TOKENS, D), jnp.float32))
    sums, stacked = lax.scan(one_expert, zeros_init, (kept_blocks, copies, router.T, picks_by_expert))
    grads, router_rows = stacked
    master_new = masters - LEARN_RATE * grads
    score_new = scores - SCORE_RATE * lax.optimization_barrier(jnp.sum(masters * grads, axis=-1))
    return (sums[0].astype(jnp.bfloat16), sums[1].astype(jnp.bfloat16), master_new, score_new, router_rows.T)
```

```python
import functools

import jax
import jax.numpy as jnp
from jax import lax
from jax.experimental import pallas as pl
from jax.experimental.pallas import tpu as pltpu
from jax.sharding import PartitionSpec as P

FF = 768
BS = 64
LANES = 2 * BS

LEARN_RATE = 0.005
SCORE_RATE = 0.05

F32 = jnp.float32
BF16 = jnp.bfloat16


def dot(a, b, dims=((1,), (0,))):
    return lax.dot_general(a, b, (dims, ((), ())), preferred_element_type=F32)


def sigma(v):
    return 1.0 / (1.0 + jnp.exp(-v))


def kernel(
    sizes,
    place_ref,
    pick_ref,
    picks_col,
    picks_row,
    tokens,
    out_grad,
    router,
    own,
    layer_out,
    input_grad,
    grads,
    router_out,
    held,
    stage,
    w_gate,
    w_up,
    w_down,
    dense,
    got,
    x_send,
    x_got,
    y_send,
    y_got,
    rows,
    scaled,
    hidden,
    pre_gate,
    pre_up,
    outs,
    r_send,
    r_got,
    w_ssem,
    w_rsem,
    g_ssem,
    g_rsem,
    x_ssem,
    x_rsem,
    y_ssem,
    y_rsem,
    r_ssem,
    r_rsem,
):
    n_dp, n_ex, members, cap = sizes
    width = tokens.shape[1]
    in_blocks = width // BS
    hid_blocks = FF // BS
    blocks = in_blocks * hid_blocks
    pairs = own.shape[1]
    total_pairs = pairs * n_dp
    slots = 2 * total_pairs
    per_peer = members * cap
    all_rows = n_ex * per_peer
    expert_rows = n_ex * cap
    my_dp = lax.axis_index("dp")
    my_ex = lax.axis_index("expert")

    def ahead(i):
        return lax.rem(my_dp + i, n_dp)

    def behind(i):
        return lax.rem(my_dp + n_dp - i, n_dp)

    def peer(i):
        return lax.rem(my_ex + i, n_ex)

    def source(i):
        return lax.rem(my_ex + n_ex - i, n_ex)

    def loop(lo, hi, fn):
        def step(i, carry):
            fn(i)
            return carry

        lax.fori_loop(lo, hi, step, 0)

    barrier = pltpu.get_barrier_semaphore()
    for i in range(1, n_dp):
        pl.semaphore_signal(
            barrier, inc=1, device_id={"dp": ahead(i)}, device_id_type=pl.DeviceIdType.MESH
        )
    loop(
        1,
        n_ex,
        lambda i: pl.semaphore_signal(
            barrier, inc=1, device_id={"expert": peer(i)}, device_id_type=pl.DeviceIdType.MESH
        ),
    )

    chosen = (
        lax.broadcasted_iota(jnp.int32, (all_rows, tokens.shape[0]), 1) == picks_col[...]
    ).astype(F32).astype(BF16)
    x_send[0] = dot(chosen, tokens[...]).astype(BF16).reshape(n_ex, per_peer, width)
    x_send[1] = dot(chosen, out_grad[...]).astype(BF16).reshape(n_ex, per_peer, width)
    y_send[...] = jnp.zeros(y_send.shape, BF16)
    stage[2 * total_pairs] = jnp.zeros((BS, LANES), BF16)
    dense[blocks // 2] = jnp.zeros((BS, LANES), F32)

    pl.semaphore_wait(barrier, n_dp - 1 + n_ex - 1)

    def x_copy(which, i):
        return pltpu.make_async_remote_copy(
            src_ref=x_send.at[which, peer(i)],
            dst_ref=x_got.at[which, my_ex],
            send_sem=x_ssem.at[which, i - 1],
            recv_sem=x_rsem.at[which, i - 1],
            device_id={"expert": peer(i)},
            device_id_type=pl.DeviceIdType.MESH,
        )

    def y_copy(which, i):
        return pltpu.make_async_remote_copy(
            src_ref=y_send.at[which, peer(i)],
            dst_ref=y_got.at[which, my_ex],
            send_sem=y_ssem.at[which, i - 1],
            recv_sem=y_rsem.at[which, i - 1],
            device_id={"expert": peer(i)},
            device_id_type=pl.DeviceIdType.MESH,
        )

    def w_copy(c, i):
        return pltpu.make_async_remote_copy(
            src_ref=own.at[c],
            dst_ref=held.at[c, i - 1],
            send_sem=w_ssem.at[c, i - 1],
            recv_sem=w_rsem.at[c, i - 1],
            device_id={"dp": ahead(i)},
            device_id_type=pl.DeviceIdType.MESH,
        )

    def g_copy(c, i):
        return pltpu.make_async_remote_copy(
            src_ref=held.at[c, i - 1],
            dst_ref=got.at[c, i - 1],
            send_sem=g_ssem.at[c, i - 1],
            recv_sem=g_rsem.at[c, i - 1],
            device_id={"dp": ahead(i)},
            device_id_type=pl.DeviceIdType.MESH,
        )

    def r_copy(i):
        return pltpu.make_async_remote_copy(
            src_ref=r_send,
            dst_ref=r_got.at[i - 1],
            send_sem=r_ssem.at[i - 1],
            recv_sem=r_rsem.at[i - 1],
            device_id={"dp": ahead(i)},
            device_id_type=pl.DeviceIdType.MESH,
        )

    loop(1, n_ex, lambda i: x_copy(0, i).start())
    for i in range(1, n_dp):
        w_copy(0, i).start()
    loop(1, n_ex, lambda i: x_copy(1, i).start())

    def send_weights(c):
        for i in range(1, n_dp):
            w_copy(c, i).start()

    loop(1, 3 * members, send_weights)
    for which in range(2):
        x_got[which, my_ex] = x_send[which, my_ex]

    low = lax.broadcasted_iota(jnp.int32, (BS, LANES), 1) < BS

    def load_stage(c):
        def put(base, tile):
            stage[base] = tile
            stage[total_pairs + base] = pltpu.roll(tile.astype(F32), BS, 1).astype(BF16)

        loop(0, pairs, lambda q: put(my_dp * pairs + q, own[c, q]))
        for i in range(1, n_dp):
            w_copy(c, i).wait_recv()
            loop(0, pairs, lambda q: put(behind(i) * pairs + q, held[c, i - 1, q]))

    def assemble(c, target, row_blocks, col_blocks):
        load_stage(c)

        def one_row(r):
            start = pl.multiple_of(r * BS, BS)
            for k in range(col_blocks // 2):
                at = c * blocks + r * col_blocks + 2 * k
                tile = jnp.where(low, stage[place_ref[at]], stage[place_ref[at + 1]])
                target[pl.ds(start, BS), k * LANES : (k + 1) * LANES] = tile

        loop(0, row_blocks, one_row)

    def dense_grad(left, right, row_blocks):
        height = row_blocks * BS
        step = 512 if height % 512 == 0 else height
        for col in range(0, right.shape[1], 2 * LANES):
            for row in range(0, height, step):
                product = dot(
                    left[:, row : row + step], right[:, col : col + 2 * LANES], ((0,), (0,))
                )
                for half in range(2):
                    base = (col // LANES + half) * row_blocks + row // BS
                    dense[base : base + step // BS] = product[
                        :, half * LANES : (half + 1) * LANES
                    ].reshape(step // BS, BS, LANES)

    def extract(c):
        def tile(d, q):
            at = c * slots + d * 2 * pairs + q
            code0 = pick_ref[at]
            code1 = pick_ref[at + pairs]
            first = dense[code0 // 2]
            second = dense[code1 // 2]
            side0 = jnp.full((BS, LANES), code0 % 2, jnp.int32)
            side1 = jnp.full((BS, LANES), code1 % 2, jnp.int32)
            first = jnp.where(side0 == 0, first, pltpu.roll(first, BS, 1))
            second = jnp.where(side1 == 1, second, pltpu.roll(second, BS, 1))
            return jnp.where(low, first, second)

        for i in range(1, n_dp):

            def fill(q):
                held[c, i - 1, q] = tile(ahead(i), q).astype(BF16)

            loop(0, pairs, fill)
            g_copy(c, i).start()

        def keep(q):
            grads[c, q] = tile(my_dp, q)

        loop(0, pairs, keep)

    def order(e):
        at = lax.broadcasted_iota(jnp.int32, (expert_rows, all_rows), 0)
        col = lax.broadcasted_iota(jnp.int32, (expert_rows, all_rows), 1)
        wanted = (at // cap) * per_peer + e * cap + at % cap
        return (col == wanted).astype(F32).astype(BF16)

    def order_back(e):
        col = lax.broadcasted_iota(jnp.int32, (all_rows, expert_rows), 1)
        at = lax.broadcasted_iota(jnp.int32, (all_rows, expert_rows), 0)
        wanted = (col // cap) * per_peer + e * cap + col % cap
        return (at == wanted).astype(F32).astype(BF16)

    def add_part(which, e, part):
        back = dot(order_back(e), part).reshape(n_ex, per_peer, width)
        y_send[which] = (y_send[which].astype(F32) + back).astype(BF16)

    def send_back(which):
        loop(1, n_ex, lambda i: y_copy(which, i).start())
        y_got[which, my_ex] = y_send[which, my_ex]

    def one_expert(e):
        c = 3 * e
        assemble(c, w_gate, in_blocks, hid_blocks)

        @pl.when(e == 0)
        def _():
            loop(1, n_ex, lambda i: x_copy(0, i).wait_recv())

        rows[...] = dot(order(e), x_got[0].reshape(all_rows, width)).astype(BF16)
        pre_gate[...] = dot(rows[...], w_gate[...])
        gating = sigma(
            jnp.sum(rows[...].astype(F32) * router[e], axis=1, keepdims=True)
        )
        assemble(c + 1, w_up, in_blocks, hid_blocks)
        pre_up[...] = dot(rows[...], w_up[...])
        gate = pre_gate[...]
        hidden[...] = (gate * sigma(gate) * pre_up[...]).astype(BF16)

        @pl.when(e == 0)
        def _():
            loop(1, n_ex, lambda i: x_copy(1, i).wait_recv())

        grad_rows = dot(order(e), x_got[1].reshape(all_rows, width))
        scaled[...] = (gating * grad_rows).astype(BF16)
        dense_grad(hidden, scaled, hid_blocks)
        assemble(c + 2, w_down, hid_blocks, in_blocks)
        extract(c + 2)
        outs[...] = dot(hidden[...], w_down[...])
        add_part(0, e, (gating * outs[...]).astype(BF16))
        grad_rows = dot(order(e), x_got[1].reshape(all_rows, width))
        logit = (
            jnp.sum(grad_rows * outs[...], axis=1, keepdims=True) * gating * (1.0 - gating)
        )
        r_send[e] = jnp.sum(rows[...].astype(F32) * logit, axis=0, keepdims=True)

        @pl.when(e == members - 1)
        def _():
            for i in range(1, n_dp):
                r_copy(i).start()
            send_back(0)

        hidden_grad = dot(scaled[...], w_down[...], ((1,), (1,)))
        gate = pre_gate[...]
        sig = sigma(gate)
        gate_grad = hidden_grad * pre_up[...] * sig * (1.0 + gate * (1.0 - sig))
        up_grad = hidden_grad * gate * sig
        pre_gate[...] = gate_grad
        pre_up[...] = up_grad
        dense_grad(rows, pre_gate[...].astype(BF16), in_blocks)
        extract(c)
        dense_grad(rows, pre_up[...].astype(BF16), in_blocks)
        extract(c + 1)
        part = dot(pre_gate[...].astype(BF16), w_gate[...], ((1,), (1,)))
        part = part + dot(pre_up[...].astype(BF16), w_up[...], ((1,), (1,)))
        add_part(1, e, (part + logit * router[e]).astype(BF16))

    loop(0, members, one_expert)
    send_back(1)

    placed = (
        lax.broadcasted_iota(jnp.int32, (tokens.shape[0], all_rows), 0) == picks_row[...]
    ).astype(F32).astype(BF16)
    loop(1, n_ex, lambda i: y_copy(0, i).wait_recv())
    layer_out[...] = dot(placed, y_got[0].reshape(all_rows, width)).astype(BF16)
    loop(1, n_ex, lambda i: y_copy(1, i).wait_recv())
    input_grad[...] = dot(placed, y_got[1].reshape(all_rows, width)).astype(BF16)

    for i in range(1, n_dp):
        r_copy(i).wait()
    share = width // n_dp
    mine = pl.ds(pl.multiple_of(my_dp * share, share), share)
    for e in range(members):
        router_total = r_send[e, :, mine]
        for i in range(1, n_dp):
            router_total = router_total + r_got[i - 1, e, :, mine]
        router_out[e] = router_total

    def finish(c):
        for i in range(1, n_dp):
            g_copy(c, i).wait_recv()

        def add(q):
            total = grads[c, q]
            for i in range(1, n_dp):
                total = total + got[c, i - 1, q].astype(F32)
            grads[c, q] = total

        loop(0, pairs, add)

    def finish_expert(e):
        for m in (2, 0, 1):
            finish(3 * e + m)

    loop(0, members, finish_expert)

    def drain_weights(c):
        for i in range(1, n_dp):
            w_copy(c, i).wait_send()
            g_copy(c, i).wait_send()

    loop(0, 3 * members, drain_weights)

    def drain_rows(i):
        for which in range(2):
            x_copy(which, i).wait_send()
            y_copy(which, i).wait_send()

    loop(1, n_ex, drain_rows)


def body(tokens, out_grad, token_picks, router, kept_blocks, masters, scores):
    members = kept_blocks.shape[0]
    slots = kept_blocks.shape[2]
    n_ex = lax.axis_size("expert")
    n_dp = lax.axis_size("dp")
    cap = token_picks.shape[2]
    width = tokens.shape[1]
    in_blocks = width // BS
    hid_blocks = FF // BS
    blocks = in_blocks * hid_blocks
    local = masters.shape[2]
    pairs = local // 2
    total_pairs = pairs * n_dp
    chunks = 3 * members
    all_rows = n_ex * members * cap
    expert_rows = n_ex * cap

    kept = kept_blocks.reshape(chunks, slots)
    numbers = jnp.arange(blocks, dtype=jnp.int32)
    hits = kept[:, None, :] == numbers[None, :, None]
    slot_of = jnp.sum(
        jnp.where(hits, jnp.arange(slots, dtype=jnp.int32) + 1, 0), axis=2
    ) - 1
    within = slot_of % local
    flipped = (within // pairs) != (numbers % 2)[None, :]
    place = (slot_of // local) * pairs + within % pairs + jnp.where(flipped, total_pairs, 0)
    place = jnp.where(slot_of >= 0, place, 2 * total_pairs).reshape(-1)

    col_counts = jnp.array([hid_blocks, hid_blocks, in_blocks] * members, jnp.int32)[:, None]
    row_counts = jnp.array([in_blocks, in_blocks, hid_blocks] * members, jnp.int32)[:, None]
    block_row = kept // col_counts
    block_col = kept % col_counts
    code = ((block_col // 2) * row_counts + block_row) * 2 + block_col % 2
    code = jnp.where(kept < blocks, code, blocks).reshape(-1)

    own = masters.astype(BF16).reshape(chunks, 2, pairs, BS, BS)
    own = own.transpose(0, 2, 3, 1, 4).reshape(chunks, pairs, BS, LANES)
    picks = token_picks[0].reshape(-1)
    router_rows = router.T.astype(F32).reshape(members, 1, width)

    vmem = pl.BlockSpec(memory_space=pltpu.VMEM)
    smem = pl.BlockSpec(memory_space=pltpu.SMEM)
    dma = pltpu.SemaphoreType.DMA
    layer_out, input_grad, grads, router_grad = pl.pallas_call(
        functools.partial(kernel, (n_dp, n_ex, members, cap)),
        out_shape=(
            jax.ShapeDtypeStruct(tokens.shape, BF16),
            jax.ShapeDtypeStruct(tokens.shape, BF16),
            jax.ShapeDtypeStruct((chunks, pairs, BS, LANES), F32),
            jax.ShapeDtypeStruct((members, 1, width // n_dp), F32),
        ),
        in_specs=[smem, smem] + [vmem] * 6,
        out_specs=[vmem] * 4,
        scratch_shapes=[
            pltpu.VMEM((chunks, n_dp - 1, pairs, BS, LANES), BF16),
            pltpu.VMEM((2 * total_pairs + 1, BS, LANES), BF16),
            pltpu.VMEM((width, FF), BF16),
            pltpu.VMEM((width, FF), BF16),
            pltpu.VMEM((FF, width), BF16),
            pltpu.VMEM((blocks // 2 + 1, BS, LANES), F32),
            pltpu.VMEM((chunks, n_dp - 1, pairs, BS, LANES), BF16),
            pltpu.VMEM((2, n_ex, members * cap, width), BF16),
            pltpu.VMEM((2, n_ex, members * cap, width), BF16),
            pltpu.VMEM((2, n_ex, members * cap, width), BF16),
            pltpu.VMEM((2, n_ex, members * cap, width), BF16),
            pltpu.VMEM((expert_rows, width), BF16),
            pltpu.VMEM((expert_rows, width), BF16),
            pltpu.VMEM((expert_rows, FF), BF16),
            pltpu.VMEM((expert_rows, FF), F32),
            pltpu.VMEM((expert_rows, FF), F32),
            pltpu.VMEM((expert_rows, width), F32),
            pltpu.VMEM((members, 1, width), F32),
            pltpu.VMEM((n_dp - 1, members, 1, width), F32),
            dma((chunks, n_dp - 1)),
            dma((chunks, n_dp - 1)),
            dma((chunks, n_dp - 1)),
            dma((chunks, n_dp - 1)),
            dma((2, n_ex - 1)),
            dma((2, n_ex - 1)),
            dma((2, n_ex - 1)),
            dma((2, n_ex - 1)),
            dma((n_dp - 1,)),
            dma((n_dp - 1,)),
        ],
        compiler_params=pltpu.CompilerParams(
            collective_id=0, has_side_effects=True, vmem_limit_bytes=62 * 1024 * 1024
        ),
    )(
        place,
        code,
        picks.reshape(all_rows, 1),
        picks.reshape(1, all_rows),
        tokens,
        out_grad,
        router_rows,
        own,
    )

    summed = grads.reshape(members, 3, pairs, BS, 2, BS).transpose(0, 1, 4, 2, 3, 5)
    summed = summed.reshape(members, 3, local, BS * BS)
    master_new = masters - LEARN_RATE * summed
    score_new = scores - SCORE_RATE * jnp.sum(masters * summed, axis=-1)
    return layer_out, input_grad, master_new, score_new, router_grad.reshape(members, -1).T


def solution(mesh):
    return jax.shard_map(
        body,
        mesh=mesh,
        in_specs=(
            P(("dp", "expert"), None),
            P(("dp", "expert"), None),
            P(("dp", "expert"), None, None),
            P(None, "expert"),
            P("expert", None, None),
            P("expert", None, "dp", None),
            P("expert", None, "dp"),
        ),
        out_specs=(
            P(("dp", "expert"), None),
            P(("dp", "expert"), None),
            P("expert", None, "dp", None),
            P("expert", None, "dp"),
            P("dp", "expert"),
        ),
        check_vma=False,
    )
```

```python
import functools

import jax
import jax.numpy as jnp
from jax import lax
from jax.experimental import pallas as pl
from jax.experimental.pallas import tpu as pltpu
from jax.sharding import PartitionSpec as P

FF = 768
BS = 64
LANES = 2 * BS

LEARN_RATE = 0.005
SCORE_RATE = 0.05

F32 = jnp.float32
BF16 = jnp.bfloat16


def dot(a, b, dims=((1,), (0,))):
    return lax.dot_general(a, b, (dims, ((), ())), preferred_element_type=F32)


def sigma(v):
    return 1.0 / (1.0 + jnp.exp(-v))


def kernel(
    sizes,
    place_ref,
    pick_ref,
    picks_col,
    picks_row,
    tokens,
    out_grad,
    router,
    masters,
    layer_out,
    input_grad,
    master_new,
    score_sum,
    router_out,
    own,
    paired,
    tiles,
    held,
    stage,
    w_gate,
    w_up,
    w_down,
    dense,
    got,
    x_send,
    x_got,
    y_got,
    rows,
    scaled,
    hidden,
    pre_gate,
    pre_up,
    outs,
    r_send,
    r_got,
    w_ssem,
    w_rsem,
    g_ssem,
    g_rsem,
    x_ssem,
    x_rsem,
    y_ssem,
    y_rsem,
    r_ssem,
    r_rsem,
):
    n_dp, n_ex, members, cap = sizes
    width = tokens.shape[1]
    in_blocks = width // BS
    hid_blocks = FF // BS
    blocks = in_blocks * hid_blocks
    pairs = masters.shape[1] // 2
    total_pairs = pairs * n_dp
    slots = 2 * total_pairs
    per_peer = members * cap
    all_rows = n_ex * per_peer
    expert_rows = n_ex * cap
    my_dp = lax.axis_index("dp")
    my_ex = lax.axis_index("expert")

    def ahead(i):
        return lax.rem(my_dp + i, n_dp)

    def behind(i):
        return lax.rem(my_dp + n_dp - i, n_dp)

    def peer(i):
        return lax.rem(my_ex + i, n_ex)

    def source(i):
        return lax.rem(my_ex + n_ex - i, n_ex)

    def loop(lo, hi, fn):
        def step(i, carry):
            fn(i)
            return carry

        lax.fori_loop(lo, hi, step, 0)

    barrier = pltpu.get_barrier_semaphore()
    for i in range(1, n_dp):
        pl.semaphore_signal(
            barrier, inc=1, device_id={"dp": ahead(i)}, device_id_type=pl.DeviceIdType.MESH
        )
    loop(
        1,
        n_ex,
        lambda i: pl.semaphore_signal(
            barrier, inc=1, device_id={"expert": peer(i)}, device_id_type=pl.DeviceIdType.MESH
        ),
    )

    chosen = (
        lax.broadcasted_iota(jnp.int32, (all_rows, tokens.shape[0]), 1) == picks_col[...]
    ).astype(F32).astype(BF16)
    x_send[0] = dot(chosen, tokens[...]).astype(BF16).reshape(n_ex, per_peer, width)
    x_send[1] = dot(chosen, out_grad[...]).astype(BF16).reshape(n_ex, per_peer, width)
    stage[2 * total_pairs] = jnp.zeros((BS, LANES), BF16)
    dense[blocks // 2] = jnp.zeros((BS, LANES), F32)

    half_low = lax.broadcasted_iota(jnp.int32, (BS // 2, LANES), 1) < BS
    half = BS // 2

    def pack(c):
        for j in range(half):
            paired[pl.ds(j, 2 * pairs, stride=half), :] = masters[c, :, j * LANES : (j + 1) * LANES]

        def interleave(q):
            first = paired[pl.ds(pl.multiple_of(q * half, half), half), :]
            second = paired[pl.ds(pl.multiple_of((q + pairs) * half, half), half), :]
            tiles[pl.ds(q * BS, half, stride=2), :] = jnp.where(
                half_low, first, pltpu.roll(second, BS, 1)
            )
            tiles[pl.ds(q * BS + 1, half, stride=2), :] = jnp.where(
                half_low, pltpu.roll(first, BS, 1), second
            )

        loop(0, pairs, interleave)

        def narrow(q):
            own[c, q] = tiles[pl.ds(pl.multiple_of(q * BS, BS), BS), :].astype(BF16)

        loop(0, pairs, narrow)

    pack(0)
    pl.semaphore_wait(barrier, n_dp - 1 + n_ex - 1)

    def x_copy(which, i):
        return pltpu.make_async_remote_copy(
            src_ref=x_send.at[which, peer(i)],
            dst_ref=x_got.at[which, my_ex],
            send_sem=x_ssem.at[which, i - 1],
            recv_sem=x_rsem.at[which, i - 1],
            device_id={"expert": peer(i)},
            device_id_type=pl.DeviceIdType.MESH,
        )

    def y_copy(which, i):
        return pltpu.make_async_remote_copy(
            src_ref=x_send.at[which, peer(i)],
            dst_ref=y_got.at[which, my_ex],
            send_sem=y_ssem.at[which, i - 1],
            recv_sem=y_rsem.at[which, i - 1],
            device_id={"expert": peer(i)},
            device_id_type=pl.DeviceIdType.MESH,
        )

    def w_copy(c, i):
        return pltpu.make_async_remote_copy(
            src_ref=own.at[c],
            dst_ref=held.at[c, i - 1],
            send_sem=w_ssem.at[c, i - 1],
            recv_sem=w_rsem.at[c, i - 1],
            device_id={"dp": ahead(i)},
            device_id_type=pl.DeviceIdType.MESH,
        )

    def g_copy(c, i):
        return pltpu.make_async_remote_copy(
            src_ref=held.at[c, i - 1],
            dst_ref=got.at[c, i - 1],
            send_sem=g_ssem.at[c, i - 1],
            recv_sem=g_rsem.at[c, i - 1],
            device_id={"dp": ahead(i)},
            device_id_type=pl.DeviceIdType.MESH,
        )

    def r_copy(i):
        return pltpu.make_async_remote_copy(
            src_ref=r_send,
            dst_ref=r_got.at[i - 1],
            send_sem=r_ssem.at[i - 1],
            recv_sem=r_rsem.at[i - 1],
            device_id={"dp": ahead(i)},
            device_id_type=pl.DeviceIdType.MESH,
        )

    loop(1, n_ex, lambda i: x_copy(0, i).start())
    for i in range(1, n_dp):
        w_copy(0, i).start()
    loop(1, n_ex, lambda i: x_copy(1, i).start())

    def send_weights(c):
        pack(c)
        for i in range(1, n_dp):
            w_copy(c, i).start()

    loop(1, 3 * members, send_weights)
    for which in range(2):
        x_got[which, my_ex] = x_send[which, my_ex]

    low = lax.broadcasted_iota(jnp.int32, (BS, LANES), 1) < BS

    def load_stage(c):
        def put(base, tile):
            stage[base] = tile
            stage[total_pairs + base] = pltpu.roll(tile.astype(F32), BS, 1).astype(BF16)

        loop(0, pairs, lambda q: put(my_dp * pairs + q, own[c, q]))
        for i in range(1, n_dp):
            w_copy(c, i).wait_recv()
            loop(0, pairs, lambda q: put(behind(i) * pairs + q, held[c, i - 1, q]))

    def assemble(c, target, row_blocks, col_blocks):
        load_stage(c)

        def one_row(r):
            start = pl.multiple_of(r * BS, BS)
            for k in range(col_blocks // 2):
                at = c * blocks + r * col_blocks + 2 * k
                tile = jnp.where(low, stage[place_ref[at]], stage[place_ref[at + 1]])
                target[pl.ds(start, BS), k * LANES : (k + 1) * LANES] = tile

        loop(0, row_blocks, one_row)

    def dense_grad(left, right, row_blocks):
        height = row_blocks * BS
        step = 512 if height % 512 == 0 else height
        for col in range(0, right.shape[1], 2 * LANES):
            for row in range(0, height, step):
                product = dot(
                    left[:, row : row + step], right[:, col : col + 2 * LANES], ((0,), (0,))
                )
                for half in range(2):
                    base = (col // LANES + half) * row_blocks + row // BS
                    dense[base : base + step // BS] = product[
                        :, half * LANES : (half + 1) * LANES
                    ].reshape(step // BS, BS, LANES)

    def extract(c):
        def tile(d, q):
            at = c * slots + d * 2 * pairs + q
            code0 = pick_ref[at]
            code1 = pick_ref[at + pairs]
            first = dense[code0 // 2]
            second = dense[code1 // 2]
            side0 = jnp.full((BS, LANES), code0 % 2, jnp.int32)
            side1 = jnp.full((BS, LANES), code1 % 2, jnp.int32)
            first = jnp.where(side0 == 0, first, pltpu.roll(first, BS, 1))
            second = jnp.where(side1 == 1, second, pltpu.roll(second, BS, 1))
            return jnp.where(low, first, second)

        for i in range(1, n_dp):

            def fill(q):
                held[c, i - 1, q] = tile(ahead(i), q).astype(BF16)

            loop(0, pairs, fill)
            g_copy(c, i).start()

        for i in range(1, n_dp):
            w_copy(c, i).wait_send()

        def keep(q):
            own[c, q] = tile(my_dp, q).astype(BF16)

        loop(0, pairs, keep)

    def order(e):
        at = lax.broadcasted_iota(jnp.int32, (expert_rows, all_rows), 0)
        col = lax.broadcasted_iota(jnp.int32, (expert_rows, all_rows), 1)
        wanted = (at // cap) * per_peer + e * cap + at % cap
        return (col == wanted).astype(F32).astype(BF16)

    def order_back(e):
        col = lax.broadcasted_iota(jnp.int32, (all_rows, expert_rows), 1)
        at = lax.broadcasted_iota(jnp.int32, (all_rows, expert_rows), 0)
        wanted = (col // cap) * per_peer + e * cap + col % cap
        return (at == wanted).astype(F32).astype(BF16)

    def add_part(which, e, part):
        back = dot(order_back(e), part).reshape(n_ex, per_peer, width)
        x_send[which] = (x_send[which].astype(F32) + back).astype(BF16)

    def send_back(which):
        loop(1, n_ex, lambda i: y_copy(which, i).start())
        y_got[which, my_ex] = x_send[which, my_ex]

    def one_expert(e):
        c = 3 * e
        assemble(c, w_gate, in_blocks, hid_blocks)

        @pl.when(e == 0)
        def _():
            loop(1, n_ex, lambda i: x_copy(0, i).wait_recv())

        rows[...] = dot(order(e), x_got[0].reshape(all_rows, width)).astype(BF16)
        pre_gate[...] = dot(rows[...], w_gate[...])
        gating = sigma(
            jnp.sum(rows[...].astype(F32) * router[e], axis=1, keepdims=True)
        )
        assemble(c + 1, w_up, in_blocks, hid_blocks)
        pre_up[...] = dot(rows[...], w_up[...])
        gate = pre_gate[...]
        hidden[...] = (gate * sigma(gate) * pre_up[...]).astype(BF16)

        @pl.when(e == 0)
        def _():
            loop(1, n_ex, lambda i: x_copy(1, i).wait_recv())

            def sent(i):
                for which in range(2):
                    x_copy(which, i).wait_send()

            loop(1, n_ex, sent)
            x_send[...] = jnp.zeros(x_send.shape, BF16)

        grad_rows = dot(order(e), x_got[1].reshape(all_rows, width))
        scaled[...] = (gating * grad_rows).astype(BF16)
        dense_grad(hidden, scaled, hid_blocks)
        assemble(c + 2, w_down, hid_blocks, in_blocks)
        extract(c + 2)
        outs[...] = dot(hidden[...], w_down[...])
        add_part(0, e, (gating * outs[...]).astype(BF16))
        grad_rows = dot(order(e), x_got[1].reshape(all_rows, width))
        logit = (
            jnp.sum(grad_rows * outs[...], axis=1, keepdims=True) * gating * (1.0 - gating)
        )
        r_send[e] = jnp.sum(rows[...].astype(F32) * logit, axis=0, keepdims=True)

        @pl.when(e == members - 1)
        def _():
            for i in range(1, n_dp):
                r_copy(i).start()
            send_back(0)

        hidden_grad = dot(scaled[...], w_down[...], ((1,), (1,)))
        gate = pre_gate[...]
        sig = sigma(gate)
        gate_grad = hidden_grad * pre_up[...] * sig * (1.0 + gate * (1.0 - sig))
        up_grad = hidden_grad * gate * sig
        pre_gate[...] = gate_grad
        pre_up[...] = up_grad
        dense_grad(rows, pre_gate[...].astype(BF16), in_blocks)
        extract(c)
        dense_grad(rows, pre_up[...].astype(BF16), in_blocks)
        extract(c + 1)
        part = dot(pre_gate[...].astype(BF16), w_gate[...], ((1,), (1,)))
        part = part + dot(pre_up[...].astype(BF16), w_up[...], ((1,), (1,)))
        add_part(1, e, (part + logit * router[e]).astype(BF16))

    loop(0, members, one_expert)
    send_back(1)

    def finish(c):
        for i in range(1, n_dp):
            g_copy(c, i).wait_recv()

        def add(q):
            total = own[c, q].astype(F32)
            for i in range(1, n_dp):
                total = total + got[c, i - 1, q].astype(F32)
            tiles[pl.ds(pl.multiple_of(q * BS, BS), BS), :] = total

        loop(0, pairs, add)

        def separate(q):
            even = tiles[pl.ds(q * BS, half, stride=2), :]
            odd = tiles[pl.ds(q * BS + 1, half, stride=2), :]
            paired[pl.ds(pl.multiple_of(q * half, half), half), :] = jnp.where(
                half_low, even, pltpu.roll(odd, BS, 1)
            )
            paired[pl.ds(pl.multiple_of((q + pairs) * half, half), half), :] = jnp.where(
                half_low, pltpu.roll(even, BS, 1), odd
            )

        loop(0, pairs, separate)
        score = jnp.zeros((2 * pairs, LANES), F32)
        for j in range(half):
            part = paired[pl.ds(j, 2 * pairs, stride=half), :]
            master = masters[c, :, j * LANES : (j + 1) * LANES]
            master_new[c, :, j * LANES : (j + 1) * LANES] = master - LEARN_RATE * part
            score = score + master * part
        score_sum[c] = jnp.sum(score, axis=1, keepdims=True)

    def finish_expert(e):
        for m in (2, 0, 1):
            finish(3 * e + m)

    loop(0, members - 1, finish_expert)
    placed = (
        lax.broadcasted_iota(jnp.int32, (tokens.shape[0], all_rows), 0) == picks_row[...]
    ).astype(F32).astype(BF16)
    loop(1, n_ex, lambda i: y_copy(0, i).wait_recv())
    layer_out[...] = dot(placed, y_got[0].reshape(all_rows, width)).astype(BF16)
    loop(1, n_ex, lambda i: y_copy(1, i).wait_recv())
    input_grad[...] = dot(placed, y_got[1].reshape(all_rows, width)).astype(BF16)

    for i in range(1, n_dp):
        r_copy(i).wait()
    share = width // n_dp
    mine = pl.ds(pl.multiple_of(my_dp * share, share), share)
    for e in range(members):
        router_total = r_send[e, :, mine]
        for i in range(1, n_dp):
            router_total = router_total + r_got[i - 1, e, :, mine]
        router_out[e] = router_total

    finish_expert(members - 1)

    def drain_weights(c):
        for i in range(1, n_dp):
            g_copy(c, i).wait_send()

    loop(0, 3 * members, drain_weights)

    def drain_rows(i):
        for which in range(2):
            y_copy(which, i).wait_send()

    loop(1, n_ex, drain_rows)


def body(tokens, out_grad, token_picks, router, kept_blocks, masters, scores):
    members = kept_blocks.shape[0]
    slots = kept_blocks.shape[2]
    n_ex = lax.axis_size("expert")
    n_dp = lax.axis_size("dp")
    cap = token_picks.shape[2]
    width = tokens.shape[1]
    in_blocks = width // BS
    hid_blocks = FF // BS
    blocks = in_blocks * hid_blocks
    local = masters.shape[2]
    pairs = local // 2
    total_pairs = pairs * n_dp
    chunks = 3 * members
    all_rows = n_ex * members * cap
    expert_rows = n_ex * cap

    kept = kept_blocks.reshape(chunks, slots)
    numbers = jnp.arange(blocks, dtype=jnp.int32)
    hits = kept[:, None, :] == numbers[None, :, None]
    slot_of = jnp.sum(
        jnp.where(hits, jnp.arange(slots, dtype=jnp.int32) + 1, 0), axis=2
    ) - 1
    within = slot_of % local
    flipped = (within // pairs) != (numbers % 2)[None, :]
    place = (slot_of // local) * pairs + within % pairs + jnp.where(flipped, total_pairs, 0)
    place = jnp.where(slot_of >= 0, place, 2 * total_pairs).reshape(-1)

    col_counts = jnp.array([hid_blocks, hid_blocks, in_blocks] * members, jnp.int32)[:, None]
    row_counts = jnp.array([in_blocks, in_blocks, hid_blocks] * members, jnp.int32)[:, None]
    block_row = kept // col_counts
    block_col = kept % col_counts
    code = ((block_col // 2) * row_counts + block_row) * 2 + block_col % 2
    code = jnp.where(kept < blocks, code, blocks).reshape(-1)

    picks = token_picks[0].reshape(-1)
    router_rows = router.T.astype(F32).reshape(members, 1, width)

    vmem = pl.BlockSpec(memory_space=pltpu.VMEM)
    smem = pl.BlockSpec(memory_space=pltpu.SMEM)
    dma = pltpu.SemaphoreType.DMA
    layer_out, input_grad, master_new, score_sum, router_grad = pl.pallas_call(
        functools.partial(kernel, (n_dp, n_ex, members, cap)),
        out_shape=(
            jax.ShapeDtypeStruct(tokens.shape, BF16),
            jax.ShapeDtypeStruct(tokens.shape, BF16),
            jax.ShapeDtypeStruct((chunks, local, BS * BS), F32),
            jax.ShapeDtypeStruct((chunks, local, 1), F32),
            jax.ShapeDtypeStruct((members, 1, width // n_dp), F32),
        ),
        in_specs=[smem, smem] + [vmem] * 6,
        out_specs=[vmem] * 5,
        scratch_shapes=[
            pltpu.VMEM((chunks, pairs, BS, LANES), BF16),
            pltpu.VMEM((local * BS // 2, LANES), F32),
            pltpu.VMEM((pairs * BS, LANES), F32),
            pltpu.VMEM((chunks, n_dp - 1, pairs, BS, LANES), BF16),
            pltpu.VMEM((2 * total_pairs + 1, BS, LANES), BF16),
            pltpu.VMEM((width, FF), BF16),
            pltpu.VMEM((width, FF), BF16),
            pltpu.VMEM((FF, width), BF16),
            pltpu.VMEM((blocks // 2 + 1, BS, LANES), F32),
            pltpu.VMEM((chunks, n_dp - 1, pairs, BS, LANES), BF16),
            pltpu.VMEM((2, n_ex, members * cap, width), BF16),
            pltpu.VMEM((2, n_ex, members * cap, width), BF16),
            pltpu.VMEM((2, n_ex, members * cap, width), BF16),
            pltpu.VMEM((expert_rows, width), BF16),
            pltpu.VMEM((expert_rows, width), BF16),
            pltpu.VMEM((expert_rows, FF), BF16),
            pltpu.VMEM((expert_rows, FF), F32),
            pltpu.VMEM((expert_rows, FF), F32),
            pltpu.VMEM((expert_rows, width), F32),
            pltpu.VMEM((members, 1, width), F32),
            pltpu.VMEM((n_dp - 1, members, 1, width), F32),
            dma((chunks, n_dp - 1)),
            dma((chunks, n_dp - 1)),
            dma((chunks, n_dp - 1)),
            dma((chunks, n_dp - 1)),
            dma((2, n_ex - 1)),
            dma((2, n_ex - 1)),
            dma((2, n_ex - 1)),
            dma((2, n_ex - 1)),
            dma((n_dp - 1,)),
            dma((n_dp - 1,)),
        ],
        compiler_params=pltpu.CompilerParams(
            collective_id=0, has_side_effects=True, vmem_limit_bytes=62 * 1024 * 1024
        ),
    )(
        place,
        code,
        picks.reshape(all_rows, 1),
        picks.reshape(1, all_rows),
        tokens,
        out_grad,
        router_rows,
        masters.reshape(chunks, local, BS * BS),
    )

    master_new = master_new.reshape(masters.shape)
    score_new = scores - SCORE_RATE * score_sum.reshape(scores.shape)
    return layer_out, input_grad, master_new, score_new, router_grad.reshape(members, -1).T


def solution(mesh):
    return jax.shard_map(
        body,
        mesh=mesh,
        in_specs=(
            P(("dp", "expert"), None),
            P(("dp", "expert"), None),
            P(("dp", "expert"), None, None),
            P(None, "expert"),
            P("expert", None, None),
            P("expert", None, "dp", None),
            P("expert", None, "dp"),
        ),
        out_specs=(
            P(("dp", "expert"), None),
            P(("dp", "expert"), None),
            P("expert", None, "dp", None),
            P("expert", None, "dp"),
            P("dp", "expert"),
        ),
        check_vma=False,
    )
```

```python
import functools

import jax
import jax.numpy as jnp
from jax import lax
from jax.experimental import pallas as pl
from jax.experimental.pallas import tpu as pltpu
from jax.sharding import PartitionSpec as P

FF = 768
BS = 64
LANES = 2 * BS

LEARN_RATE = 0.005
SCORE_RATE = 0.05

F32 = jnp.float32
BF16 = jnp.bfloat16


def dot(a, b, dims=((1,), (0,))):
    return lax.dot_general(a, b, (dims, ((), ())), preferred_element_type=F32)


def sigma(v):
    return 1.0 / (1.0 + jnp.exp(-v))


def kernel(
    sizes,
    place_ref,
    pick_ref,
    picks_col,
    picks_row,
    tokens,
    out_grad,
    router,
    masters,
    layer_out,
    input_grad,
    master_new,
    score_sum,
    router_out,
    own,
    paired,
    tiles,
    held,
    stage,
    w_gate,
    w_up,
    w_down,
    dense,
    got,
    relay,
    x_send,
    x_got,
    y_got,
    rows,
    scaled,
    hidden,
    pre_gate,
    pre_up,
    outs,
    r_send,
    r_got,
    w_ssem,
    w_rsem,
    g_ssem,
    g_rsem,
    x_ssem,
    x_rsem,
    y_ssem,
    y_rsem,
    r_ssem,
    r_rsem,
):
    n_dp, n_ex, members, cap = sizes
    width = tokens.shape[1]
    in_blocks = width // BS
    hid_blocks = FF // BS
    blocks = in_blocks * hid_blocks
    pairs = masters.shape[1] // 2
    total_pairs = pairs * n_dp
    slots = 2 * total_pairs
    per_peer = members * cap
    all_rows = n_ex * per_peer
    expert_rows = n_ex * cap
    my_dp = lax.axis_index("dp")
    my_ex = lax.axis_index("expert")

    def ahead(i):
        return lax.rem(my_dp + i, n_dp)

    near_a = my_dp + 1 - 2 * (my_dp % 2)
    near_b = my_dp + 2 - 4 * (my_dp // 2)
    across = n_dp - 1 - my_dp

    def peer(i):
        return lax.rem(my_ex + i, n_ex)

    def loop(lo, hi, fn):
        def step(i, carry):
            fn(i)
            return carry

        lax.fori_loop(lo, hi, step, 0)

    barrier = pltpu.get_barrier_semaphore()
    for i in range(1, n_dp):
        pl.semaphore_signal(
            barrier, inc=1, device_id={"dp": ahead(i)}, device_id_type=pl.DeviceIdType.MESH
        )
    loop(
        1,
        n_ex,
        lambda i: pl.semaphore_signal(
            barrier, inc=1, device_id={"expert": peer(i)}, device_id_type=pl.DeviceIdType.MESH
        ),
    )

    chosen = (
        lax.broadcasted_iota(jnp.int32, (all_rows, tokens.shape[0]), 1) == picks_col[...]
    ).astype(F32).astype(BF16)
    x_send[0] = dot(chosen, tokens[...]).astype(BF16).reshape(n_ex, per_peer, width)
    x_send[1] = dot(chosen, out_grad[...]).astype(BF16).reshape(n_ex, per_peer, width)
    stage[2 * total_pairs] = jnp.zeros((BS, LANES), BF16)
    dense[blocks // 2] = jnp.zeros((BS, LANES), F32)

    half_low = lax.broadcasted_iota(jnp.int32, (BS // 2, LANES), 1) < BS
    half = BS // 2

    def pack(c):
        for j in range(half):
            paired[pl.ds(j, 2 * pairs, stride=half), :] = masters[c, :, j * LANES : (j + 1) * LANES]

        def interleave(q):
            first = paired[pl.ds(pl.multiple_of(q * half, half), half), :]
            second = paired[pl.ds(pl.multiple_of((q + pairs) * half, half), half), :]
            tiles[pl.ds(q * BS, half, stride=2), :] = jnp.where(
                half_low, first, pltpu.roll(second, BS, 1)
            )
            tiles[pl.ds(q * BS + 1, half, stride=2), :] = jnp.where(
                half_low, pltpu.roll(first, BS, 1), second
            )

        loop(0, pairs, interleave)

        def narrow(q):
            own[c, q] = tiles[pl.ds(pl.multiple_of(q * BS, BS), BS), :].astype(BF16)

        loop(0, pairs, narrow)

    pack(0)
    pl.semaphore_wait(barrier, n_dp - 1 + n_ex - 1)

    def x_copy(which, i):
        return pltpu.make_async_remote_copy(
            src_ref=x_send.at[which, peer(i)],
            dst_ref=x_got.at[which, my_ex],
            send_sem=x_ssem.at[which, i - 1],
            recv_sem=x_rsem.at[which, i - 1],
            device_id={"expert": peer(i)},
            device_id_type=pl.DeviceIdType.MESH,
        )

    def y_copy(which, i):
        return pltpu.make_async_remote_copy(
            src_ref=x_send.at[which, peer(i)],
            dst_ref=y_got.at[which, my_ex],
            send_sem=y_ssem.at[which, i - 1],
            recv_sem=y_rsem.at[which, i - 1],
            device_id={"expert": peer(i)},
            device_id_type=pl.DeviceIdType.MESH,
        )

    first_half = pl.ds(0, pairs // 2)
    last_half = pl.ds(pairs // 2, pairs // 2)

    def dp_copy(src, dst, send_sem, recv_sem, device):
        return pltpu.make_async_remote_copy(
            src_ref=src,
            dst_ref=dst,
            send_sem=send_sem,
            recv_sem=recv_sem,
            device_id={"dp": device},
            device_id_type=pl.DeviceIdType.MESH,
        )

    def w_copy(c, k):
        src, dst, device = (
            (own.at[c], held.at[c, 0], near_a),
            (own.at[c], held.at[c, 1], near_b),
            (held.at[c, 0, first_half], held.at[c, 2, first_half], near_b),
            (held.at[c, 1, last_half], held.at[c, 2, last_half], near_a),
        )[k]
        return dp_copy(src, dst, w_ssem.at[c, k], w_rsem.at[c, k], device)

    def g_copy(c, k):
        src, dst, device = (
            (held.at[c, 2, first_half], relay.at[c, 0], near_a),
            (held.at[c, 2, last_half], relay.at[c, 1], near_b),
            (held.at[c, 0, first_half], got.at[c, 0, first_half], near_a),
            (held.at[c, 1, last_half], got.at[c, 1, last_half], near_b),
            (held.at[c, 0, last_half], got.at[c, 0, last_half], near_a),
            (held.at[c, 1, first_half], got.at[c, 1, first_half], near_b),
        )[k]
        return dp_copy(src, dst, g_ssem.at[c, k], g_rsem.at[c, k], device)

    def r_copy(i):
        return pltpu.make_async_remote_copy(
            src_ref=r_send,
            dst_ref=r_got.at[i - 1],
            send_sem=r_ssem.at[i - 1],
            recv_sem=r_rsem.at[i - 1],
            device_id={"dp": ahead(i)},
            device_id_type=pl.DeviceIdType.MESH,
        )

    def send_weights(c):
        w_copy(c, 0).start()
        w_copy(c, 1).start()

    def forward(c):
        for k in (0, 1):
            w_copy(c, k).wait_recv()
        for k in (2, 3):
            w_copy(c, k).start()

    send_weights(0)
    loop(1, n_ex, lambda i: x_copy(0, i).start())
    for c in (1, 2):
        pack(c)
        send_weights(c)
    loop(1, n_ex, lambda i: x_copy(1, i).start())
    for which in range(2):
        x_got[which, my_ex] = x_send[which, my_ex]
    loop(3, 3 * members, pack)
    forward(0)
    forward(1)
    send_weights(3)
    forward(2)
    loop(4, 3 * members, send_weights)

    low = lax.broadcasted_iota(jnp.int32, (BS, LANES), 1) < BS

    def load_stage(c):
        def put(base, tile):
            stage[base] = tile
            stage[total_pairs + base] = pltpu.roll(tile.astype(F32), BS, 1).astype(BF16)

        loop(0, pairs, lambda q: put(my_dp * pairs + q, own[c, q]))
        for k, shard in enumerate((near_a, near_b)):
            loop(0, pairs, lambda q: put(shard * pairs + q, held[c, k, q]))
        w_copy(c, 2).wait_recv()
        w_copy(c, 3).wait_recv()
        loop(0, pairs, lambda q: put(across * pairs + q, held[c, 2, q]))

    def assemble(c, target, row_blocks, col_blocks):
        load_stage(c)

        def one_row(r):
            start = pl.multiple_of(r * BS, BS)
            for k in range(col_blocks // 2):
                at = c * blocks + r * col_blocks + 2 * k
                tile = jnp.where(low, stage[place_ref[at]], stage[place_ref[at + 1]])
                target[pl.ds(start, BS), k * LANES : (k + 1) * LANES] = tile

        loop(0, row_blocks, one_row)

    def dense_grad(left, right, row_blocks):
        height = row_blocks * BS
        step = 512 if height % 512 == 0 else height
        for col in range(0, right.shape[1], 2 * LANES):
            for row in range(0, height, step):
                product = dot(
                    left[:, row : row + step], right[:, col : col + 2 * LANES], ((0,), (0,))
                )
                for half in range(2):
                    base = (col // LANES + half) * row_blocks + row // BS
                    dense[base : base + step // BS] = product[
                        :, half * LANES : (half + 1) * LANES
                    ].reshape(step // BS, BS, LANES)

    def extract(c):
        def tile(d, q):
            at = c * slots + d * 2 * pairs + q
            code0 = pick_ref[at]
            code1 = pick_ref[at + pairs]
            first = dense[code0 // 2]
            second = dense[code1 // 2]
            side0 = jnp.full((BS, LANES), code0 % 2, jnp.int32)
            side1 = jnp.full((BS, LANES), code1 % 2, jnp.int32)
            first = jnp.where(side0 == 0, first, pltpu.roll(first, BS, 1))
            second = jnp.where(side1 == 1, second, pltpu.roll(second, BS, 1))
            return jnp.where(low, first, second)

        for k in range(4):
            w_copy(c, k).wait_send()
        for k, shard in ((2, across), (0, near_a), (1, near_b)):

            def fill(q):
                held[c, k, q] = tile(shard, q).astype(BF16)

            loop(0, pairs, fill)
            for g in ((2,), (3,), (0, 1))[k]:
                g_copy(c, g).start()

        def keep(q):
            own[c, q] = tile(my_dp, q).astype(BF16)

        loop(0, pairs, keep)

    def pass_on(c):
        g_copy(c, 0).wait_recv()
        g_copy(c, 1).wait_recv()

        def add(q):
            later = q + pairs // 2
            held[c, 0, later] = (held[c, 0, later].astype(F32) + relay[c, 1, q].astype(F32)).astype(BF16)
            held[c, 1, q] = (held[c, 1, q].astype(F32) + relay[c, 0, q].astype(F32)).astype(BF16)

        loop(0, pairs // 2, add)
        g_copy(c, 4).start()
        g_copy(c, 5).start()

    def order(e):
        at = lax.broadcasted_iota(jnp.int32, (expert_rows, all_rows), 0)
        col = lax.broadcasted_iota(jnp.int32, (expert_rows, all_rows), 1)
        wanted = (at // cap) * per_peer + e * cap + at % cap
        return (col == wanted).astype(F32).astype(BF16)

    def order_back(e):
        col = lax.broadcasted_iota(jnp.int32, (all_rows, expert_rows), 1)
        at = lax.broadcasted_iota(jnp.int32, (all_rows, expert_rows), 0)
        wanted = (col // cap) * per_peer + e * cap + col % cap
        return (at == wanted).astype(F32).astype(BF16)

    def add_part(which, e, part):
        back = dot(order_back(e), part).reshape(n_ex, per_peer, width)
        x_send[which] = (x_send[which].astype(F32) + back).astype(BF16)

    def send_back(which):
        loop(1, n_ex, lambda i: y_copy(which, i).start())
        y_got[which, my_ex] = x_send[which, my_ex]

    def one_expert(e):
        c = 3 * e
        more = e < members - 1
        assemble(c, w_gate, in_blocks, hid_blocks)

        @pl.when(e > 0)
        def _():
            pass_on(c - 2)


        @pl.when(e == 0)
        def _():
            loop(1, n_ex, lambda i: x_copy(0, i).wait_recv())

        rows[...] = dot(order(e), x_got[0].reshape(all_rows, width)).astype(BF16)
        pre_gate[...] = dot(rows[...], w_gate[...])
        gating = sigma(
            jnp.sum(rows[...].astype(F32) * router[e], axis=1, keepdims=True)
        )
        assemble(c + 1, w_up, in_blocks, hid_blocks)
        pl.when(more)(lambda: forward(c + 3))
        pre_up[...] = dot(rows[...], w_up[...])
        gate = pre_gate[...]
        hidden[...] = (gate * sigma(gate) * pre_up[...]).astype(BF16)

        @pl.when(e == 0)
        def _():
            loop(1, n_ex, lambda i: x_copy(1, i).wait_recv())

            def sent(i):
                for which in range(2):
                    x_copy(which, i).wait_send()

            loop(1, n_ex, sent)
            x_send[...] = jnp.zeros(x_send.shape, BF16)

        grad_rows = dot(order(e), x_got[1].reshape(all_rows, width))
        scaled[...] = (gating * grad_rows).astype(BF16)
        dense_grad(hidden, scaled, hid_blocks)
        assemble(c + 2, w_down, hid_blocks, in_blocks)
        extract(c + 2)
        pl.when(more)(lambda: forward(c + 4))
        outs[...] = dot(hidden[...], w_down[...])
        add_part(0, e, (gating * outs[...]).astype(BF16))
        grad_rows = dot(order(e), x_got[1].reshape(all_rows, width))
        logit = (
            jnp.sum(grad_rows * outs[...], axis=1, keepdims=True) * gating * (1.0 - gating)
        )
        r_send[e] = jnp.sum(rows[...].astype(F32) * logit, axis=0, keepdims=True)

        @pl.when(e == members - 1)
        def _():
            for i in range(1, n_dp):
                r_copy(i).start()
            send_back(0)

        pl.when(more)(lambda: forward(c + 5))
        hidden_grad = dot(scaled[...], w_down[...], ((1,), (1,)))
        gate = pre_gate[...]
        sig = sigma(gate)
        gate_grad = hidden_grad * pre_up[...] * sig * (1.0 + gate * (1.0 - sig))
        up_grad = hidden_grad * gate * sig
        pre_gate[...] = gate_grad
        pre_up[...] = up_grad
        dense_grad(rows, pre_gate[...].astype(BF16), in_blocks)
        extract(c)
        pass_on(c + 2)
        dense_grad(rows, pre_up[...].astype(BF16), in_blocks)
        extract(c + 1)
        pass_on(c)
        part = dot(pre_gate[...].astype(BF16), w_gate[...], ((1,), (1,)))
        part = part + dot(pre_up[...].astype(BF16), w_up[...], ((1,), (1,)))
        add_part(1, e, (part + logit * router[e]).astype(BF16))

    loop(0, members, one_expert)
    send_back(1)
    pass_on(3 * members - 2)

    def finish(c):
        for k in range(2, 6):
            g_copy(c, k).wait_recv()

        def add(q):
            total = own[c, q].astype(F32)
            for k in range(2):
                total = total + got[c, k, q].astype(F32)
            tiles[pl.ds(pl.multiple_of(q * BS, BS), BS), :] = total

        loop(0, pairs, add)

        def separate(q):
            even = tiles[pl.ds(q * BS, half, stride=2), :]
            odd = tiles[pl.ds(q * BS + 1, half, stride=2), :]
            paired[pl.ds(pl.multiple_of(q * half, half), half), :] = jnp.where(
                half_low, even, pltpu.roll(odd, BS, 1)
            )
            paired[pl.ds(pl.multiple_of((q + pairs) * half, half), half), :] = jnp.where(
                half_low, pltpu.roll(even, BS, 1), odd
            )

        loop(0, pairs, separate)
        score = jnp.zeros((2 * pairs, LANES), F32)
        for j in range(half):
            part = paired[pl.ds(j, 2 * pairs, stride=half), :]
            master = masters[c, :, j * LANES : (j + 1) * LANES]
            master_new[c, :, j * LANES : (j + 1) * LANES] = master - LEARN_RATE * part
            score = score + master * part
        score_sum[c] = jnp.sum(score, axis=1, keepdims=True)

    def finish_expert(e):
        for m in (2, 0, 1):
            finish(3 * e + m)

    loop(0, members - 1, finish_expert)
    placed = (
        lax.broadcasted_iota(jnp.int32, (tokens.shape[0], all_rows), 0) == picks_row[...]
    ).astype(F32).astype(BF16)
    loop(1, n_ex, lambda i: y_copy(0, i).wait_recv())
    layer_out[...] = dot(placed, y_got[0].reshape(all_rows, width)).astype(BF16)
    loop(1, n_ex, lambda i: y_copy(1, i).wait_recv())
    input_grad[...] = dot(placed, y_got[1].reshape(all_rows, width)).astype(BF16)

    for i in range(1, n_dp):
        r_copy(i).wait()
    share = width // n_dp
    mine = pl.ds(pl.multiple_of(my_dp * share, share), share)
    for e in range(members):
        router_total = r_send[e, :, mine]
        for i in range(1, n_dp):
            router_total = router_total + r_got[i - 1, e, :, mine]
        router_out[e] = router_total

    finish_expert(members - 1)

    def drain_weights(c):
        for k in range(6):
            g_copy(c, k).wait_send()

    loop(0, 3 * members, drain_weights)

    def drain_rows(i):
        for which in range(2):
            y_copy(which, i).wait_send()

    loop(1, n_ex, drain_rows)


def body(tokens, out_grad, token_picks, router, kept_blocks, masters, scores):
    members = kept_blocks.shape[0]
    slots = kept_blocks.shape[2]
    n_ex = lax.axis_size("expert")
    n_dp = lax.axis_size("dp")
    cap = token_picks.shape[2]
    width = tokens.shape[1]
    in_blocks = width // BS
    hid_blocks = FF // BS
    blocks = in_blocks * hid_blocks
    local = masters.shape[2]
    pairs = local // 2
    total_pairs = pairs * n_dp
    chunks = 3 * members
    all_rows = n_ex * members * cap
    expert_rows = n_ex * cap

    kept = kept_blocks.reshape(chunks, slots)
    numbers = jnp.arange(blocks, dtype=jnp.int32)
    hits = kept[:, None, :] == numbers[None, :, None]
    slot_of = jnp.sum(
        jnp.where(hits, jnp.arange(slots, dtype=jnp.int32) + 1, 0), axis=2
    ) - 1
    within = slot_of % local
    flipped = (within // pairs) != (numbers % 2)[None, :]
    place = (slot_of // local) * pairs + within % pairs + jnp.where(flipped, total_pairs, 0)
    place = jnp.where(slot_of >= 0, place, 2 * total_pairs).reshape(-1)

    col_counts = jnp.array([hid_blocks, hid_blocks, in_blocks] * members, jnp.int32)[:, None]
    row_counts = jnp.array([in_blocks, in_blocks, hid_blocks] * members, jnp.int32)[:, None]
    block_row = kept // col_counts
    block_col = kept % col_counts
    code = ((block_col // 2) * row_counts + block_row) * 2 + block_col % 2
    code = jnp.where(kept < blocks, code, blocks).reshape(-1)

    picks = token_picks[0].reshape(-1)
    router_rows = router.T.astype(F32).reshape(members, 1, width)

    vmem = pl.BlockSpec(memory_space=pltpu.VMEM)
    smem = pl.BlockSpec(memory_space=pltpu.SMEM)
    dma = pltpu.SemaphoreType.DMA
    layer_out, input_grad, master_new, score_sum, router_grad = pl.pallas_call(
        functools.partial(kernel, (n_dp, n_ex, members, cap)),
        out_shape=(
            jax.ShapeDtypeStruct(tokens.shape, BF16),
            jax.ShapeDtypeStruct(tokens.shape, BF16),
            jax.ShapeDtypeStruct((chunks, local, BS * BS), F32),
            jax.ShapeDtypeStruct((chunks, local, 1), F32),
            jax.ShapeDtypeStruct((members, 1, width // n_dp), F32),
        ),
        in_specs=[smem, smem] + [vmem] * 6,
        out_specs=[vmem] * 5,
        scratch_shapes=[
            pltpu.VMEM((chunks, pairs, BS, LANES), BF16),
            pltpu.VMEM((local * BS // 2, LANES), F32),
            pltpu.VMEM((pairs * BS, LANES), F32),
            pltpu.VMEM((chunks, n_dp - 1, pairs, BS, LANES), BF16),
            pltpu.VMEM((2 * total_pairs + 1, BS, LANES), BF16),
            pltpu.VMEM((width, FF), BF16),
            pltpu.VMEM((width, FF), BF16),
            pltpu.VMEM((FF, width), BF16),
            pltpu.VMEM((blocks // 2 + 1, BS, LANES), F32),
            pltpu.VMEM((chunks, 2, pairs, BS, LANES), BF16),
            pltpu.VMEM((chunks, 2, pairs // 2, BS, LANES), BF16),
            pltpu.VMEM((2, n_ex, members * cap, width), BF16),
            pltpu.VMEM((2, n_ex, members * cap, width), BF16),
            pltpu.VMEM((2, n_ex, members * cap, width), BF16),
            pltpu.VMEM((expert_rows, width), BF16),
            pltpu.VMEM((expert_rows, width), BF16),
            pltpu.VMEM((expert_rows, FF), BF16),
            pltpu.VMEM((expert_rows, FF), F32),
            pltpu.VMEM((expert_rows, FF), F32),
            pltpu.VMEM((expert_rows, width), F32),
            pltpu.VMEM((members, 1, width), F32),
            pltpu.VMEM((n_dp - 1, members, 1, width), F32),
            dma((chunks, 4)),
            dma((chunks, 4)),
            dma((chunks, 6)),
            dma((chunks, 6)),
            dma((2, n_ex - 1)),
            dma((2, n_ex - 1)),
            dma((2, n_ex - 1)),
            dma((2, n_ex - 1)),
            dma((n_dp - 1,)),
            dma((n_dp - 1,)),
        ],
        compiler_params=pltpu.CompilerParams(
            collective_id=0, has_side_effects=True, vmem_limit_bytes=62 * 1024 * 1024
        ),
    )(
        place,
        code,
        picks.reshape(all_rows, 1),
        picks.reshape(1, all_rows),
        tokens,
        out_grad,
        router_rows,
        masters.reshape(chunks, local, BS * BS),
    )

    master_new = master_new.reshape(masters.shape)
    score_new = scores - SCORE_RATE * score_sum.reshape(scores.shape)
    return layer_out, input_grad, master_new, score_new, router_grad.reshape(members, -1).T


def solution(mesh):
    return jax.shard_map(
        body,
        mesh=mesh,
        in_specs=(
            P(("dp", "expert"), None),
            P(("dp", "expert"), None),
            P(("dp", "expert"), None, None),
            P(None, "expert"),
            P("expert", None, None),
            P("expert", None, "dp", None),
            P("expert", None, "dp"),
        ),
        out_specs=(
            P(("dp", "expert"), None),
            P(("dp", "expert"), None),
            P("expert", None, "dp", None),
            P("expert", None, "dp"),
            P("dp", "expert"),
        ),
        check_vma=False,
    )
```

```python
import functools

import jax
import jax.numpy as jnp
from jax import lax
from jax.experimental import pallas as pl
from jax.experimental.pallas import tpu as pltpu
from jax.sharding import PartitionSpec as P

FF = 768
BS = 64
LANES = 2 * BS

LEARN_RATE = 0.005
SCORE_RATE = 0.05

F32 = jnp.float32
BF16 = jnp.bfloat16


def dot(a, b, dims=((1,), (0,))):
    return lax.dot_general(a, b, (dims, ((), ())), preferred_element_type=F32)


def sigma(v):
    return 1.0 / (1.0 + jnp.exp(-v))


def kernel(
    sizes,
    place_ref,
    pick_ref,
    picks_col,
    picks_row,
    tokens,
    out_grad,
    router,
    masters,
    layer_out,
    input_grad,
    master_new,
    score_sum,
    router_out,
    own,
    paired,
    tiles,
    held,
    stage,
    w_gate,
    w_up,
    w_down,
    rows_t,
    hidden_t,
    scaled_t,
    inner_t,
    got,
    relay,
    x_send,
    x_got,
    y_got,
    rows,
    scaled,
    hidden,
    pre_gate,
    pre_up,
    outs,
    r_send,
    r_got,
    w_ssem,
    w_rsem,
    g_ssem,
    g_rsem,
    x_ssem,
    x_rsem,
    y_ssem,
    y_rsem,
    r_ssem,
    r_rsem,
):
    n_dp, n_ex, members, cap = sizes
    width = tokens.shape[1]
    in_blocks = width // BS
    hid_blocks = FF // BS
    blocks = in_blocks * hid_blocks
    pairs = masters.shape[1] // 2
    total_pairs = pairs * n_dp
    slots = 2 * total_pairs
    per_peer = members * cap
    all_rows = n_ex * per_peer
    expert_rows = n_ex * cap
    my_dp = lax.axis_index("dp")
    my_ex = lax.axis_index("expert")

    def ahead(i):
        return lax.rem(my_dp + i, n_dp)

    near_a = my_dp + 1 - 2 * (my_dp % 2)
    near_b = my_dp + 2 - 4 * (my_dp // 2)
    across = n_dp - 1 - my_dp

    def peer(i):
        return lax.rem(my_ex + i, n_ex)

    def loop(lo, hi, fn, unroll=1):
        def step(i, carry):
            fn(i)
            return carry

        lax.fori_loop(lo, hi, step, 0, unroll=unroll)

    barrier = pltpu.get_barrier_semaphore()
    for i in range(1, n_dp):
        pl.semaphore_signal(
            barrier, inc=1, device_id={"dp": ahead(i)}, device_id_type=pl.DeviceIdType.MESH
        )
    loop(
        1,
        n_ex,
        lambda i: pl.semaphore_signal(
            barrier, inc=1, device_id={"expert": peer(i)}, device_id_type=pl.DeviceIdType.MESH
        ),
    )

    chosen = (
        lax.broadcasted_iota(jnp.int32, (all_rows, tokens.shape[0]), 1) == picks_col[...]
    ).astype(F32).astype(BF16)
    x_send[0] = dot(chosen, tokens[...]).astype(BF16).reshape(n_ex, per_peer, width)
    x_send[1] = dot(chosen, out_grad[...]).astype(BF16).reshape(n_ex, per_peer, width)
    stage[2 * total_pairs] = jnp.zeros((BS, LANES), BF16)
    rows_t[in_blocks] = jnp.zeros((BS, expert_rows), BF16)
    hidden_t[hid_blocks] = jnp.zeros((BS, expert_rows), BF16)
    same = (
        lax.broadcasted_iota(jnp.int32, (expert_rows, expert_rows), 0)
        == lax.broadcasted_iota(jnp.int32, (expert_rows, expert_rows), 1)
    ).astype(F32).astype(BF16)

    def turned(value):
        return dot(value, same, ((0,), (0,))).astype(BF16).reshape(-1, BS, expert_rows)


    half_low = lax.broadcasted_iota(jnp.int32, (BS // 2, LANES), 1) < BS
    half = BS // 2

    def pack(c):
        for j in range(half):
            paired[pl.ds(j, 2 * pairs, stride=half), :] = masters[c, :, j * LANES : (j + 1) * LANES]

        def interleave(q):
            first = paired[pl.ds(pl.multiple_of(q * half, half), half), :]
            second = paired[pl.ds(pl.multiple_of((q + pairs) * half, half), half), :]
            tiles[pl.ds(q * BS, half, stride=2), :] = jnp.where(
                half_low, first, pltpu.roll(second, BS, 1)
            )
            tiles[pl.ds(q * BS + 1, half, stride=2), :] = jnp.where(
                half_low, pltpu.roll(first, BS, 1), second
            )

        loop(0, pairs, interleave, 4)

        def narrow(q):
            own[c, q] = tiles[pl.ds(pl.multiple_of(q * BS, BS), BS), :].astype(BF16)

        loop(0, pairs, narrow, 4)

    pack(0)
    pl.semaphore_wait(barrier, n_dp - 1 + n_ex - 1)

    def x_copy(which, i):
        return pltpu.make_async_remote_copy(
            src_ref=x_send.at[which, peer(i)],
            dst_ref=x_got.at[which, my_ex],
            send_sem=x_ssem.at[which, i - 1],
            recv_sem=x_rsem.at[which, i - 1],
            device_id={"expert": peer(i)},
            device_id_type=pl.DeviceIdType.MESH,
        )

    def y_copy(which, i):
        return pltpu.make_async_remote_copy(
            src_ref=x_send.at[which, peer(i)],
            dst_ref=y_got.at[which, my_ex],
            send_sem=y_ssem.at[which, i - 1],
            recv_sem=y_rsem.at[which, i - 1],
            device_id={"expert": peer(i)},
            device_id_type=pl.DeviceIdType.MESH,
        )

    first_half = pl.ds(0, pairs // 2)
    last_half = pl.ds(pairs // 2, pairs // 2)

    def dp_copy(src, dst, send_sem, recv_sem, device):
        return pltpu.make_async_remote_copy(
            src_ref=src,
            dst_ref=dst,
            send_sem=send_sem,
            recv_sem=recv_sem,
            device_id={"dp": device},
            device_id_type=pl.DeviceIdType.MESH,
        )

    def w_copy(c, k):
        src, dst, device = (
            (own.at[c], held.at[c, 0], near_a),
            (own.at[c], held.at[c, 1], near_b),
            (held.at[c, 0, first_half], held.at[c, 2, first_half], near_b),
            (held.at[c, 1, last_half], held.at[c, 2, last_half], near_a),
        )[k]
        return dp_copy(src, dst, w_ssem.at[c, k], w_rsem.at[c, k], device)

    def g_copy(c, k):
        src, dst, device = (
            (held.at[c, 2, first_half], relay.at[c, 0], near_a),
            (held.at[c, 2, last_half], relay.at[c, 1], near_b),
            (held.at[c, 0, first_half], got.at[c, 0, first_half], near_a),
            (held.at[c, 1, last_half], got.at[c, 1, last_half], near_b),
            (held.at[c, 0, last_half], got.at[c, 0, last_half], near_a),
            (held.at[c, 1, first_half], got.at[c, 1, first_half], near_b),
        )[k]
        return dp_copy(src, dst, g_ssem.at[c, k], g_rsem.at[c, k], device)

    def r_copy(i):
        return pltpu.make_async_remote_copy(
            src_ref=r_send,
            dst_ref=r_got.at[i - 1],
            send_sem=r_ssem.at[i - 1],
            recv_sem=r_rsem.at[i - 1],
            device_id={"dp": ahead(i)},
            device_id_type=pl.DeviceIdType.MESH,
        )

    def send_weights(c):
        w_copy(c, 0).start()
        w_copy(c, 1).start()

    def forward(c):
        for k in (0, 1):
            w_copy(c, k).wait_recv()
        for k in (2, 3):
            w_copy(c, k).start()

    send_weights(0)
    loop(1, n_ex, lambda i: x_copy(0, i).start())
    for c in (1, 2):
        pack(c)
        send_weights(c)
    loop(1, n_ex, lambda i: x_copy(1, i).start())
    for which in range(2):
        x_got[which, my_ex] = x_send[which, my_ex]
    loop(3, 3 * members, pack)
    forward(0)
    forward(1)
    send_weights(3)
    forward(2)
    loop(4, 3 * members, send_weights)

    low = lax.broadcasted_iota(jnp.int32, (BS, LANES), 1) < BS

    def load_stage(c):
        def put(base, tile):
            stage[base] = tile
            stage[total_pairs + base] = pltpu.roll(tile.astype(F32), BS, 1).astype(BF16)

        loop(0, pairs, lambda q: put(my_dp * pairs + q, own[c, q]), 4)
        for k, shard in enumerate((near_a, near_b)):
            loop(0, pairs, lambda q: put(shard * pairs + q, held[c, k, q]), 4)
        w_copy(c, 2).wait_recv()
        w_copy(c, 3).wait_recv()
        loop(0, pairs, lambda q: put(across * pairs + q, held[c, 2, q]), 4)

    def assemble(c, target, row_blocks, col_blocks):
        load_stage(c)

        def one_row(r):
            start = pl.multiple_of(r * BS, BS)
            for k in range(col_blocks // 2):
                at = c * blocks + r * col_blocks + 2 * k
                tile = jnp.where(low, stage[place_ref[at]], stage[place_ref[at + 1]])
                target[pl.ds(start, BS), k * LANES : (k + 1) * LANES] = tile

        loop(0, row_blocks, one_row, 2)

    def extract(c, left, right):
        def slot(at):
            code = pick_ref[at]
            return left[code // BS], right[code % BS]

        def tile(d, q):
            at = c * slots + d * 2 * pairs + q
            left0, right0 = slot(at)
            left1, right1 = slot(at + pairs)
            both = dot(
                jnp.concatenate([left0, left1], axis=0),
                jnp.concatenate([right0, right1], axis=0),
                ((1,), (1,)),
            )
            return jnp.where(low, both[:BS], both[BS:])

        for k in range(4):
            w_copy(c, k).wait_send()
        for k, shard in ((2, across), (0, near_a), (1, near_b)):

            def fill(q):
                held[c, k, q] = tile(shard, q).astype(BF16)

            loop(0, pairs, fill, 4)
            for g in ((2,), (3,), (0, 1))[k]:
                g_copy(c, g).start()

        def keep(q):
            own[c, q] = tile(my_dp, q).astype(BF16)

        loop(0, pairs, keep, 4)

    def pass_on(c):
        g_copy(c, 0).wait_recv()
        g_copy(c, 1).wait_recv()

        def add(q):
            later = q + pairs // 2
            held[c, 0, later] = (held[c, 0, later].astype(F32) + relay[c, 1, q].astype(F32)).astype(BF16)
            held[c, 1, q] = (held[c, 1, q].astype(F32) + relay[c, 0, q].astype(F32)).astype(BF16)

        loop(0, pairs // 2, add, 4)
        g_copy(c, 4).start()
        g_copy(c, 5).start()

    def order(e):
        at = lax.broadcasted_iota(jnp.int32, (expert_rows, all_rows), 0)
        col = lax.broadcasted_iota(jnp.int32, (expert_rows, all_rows), 1)
        wanted = (at // cap) * per_peer + e * cap + at % cap
        return (col == wanted).astype(F32).astype(BF16)

    def order_back(e):
        col = lax.broadcasted_iota(jnp.int32, (all_rows, expert_rows), 1)
        at = lax.broadcasted_iota(jnp.int32, (all_rows, expert_rows), 0)
        wanted = (col // cap) * per_peer + e * cap + col % cap
        return (at == wanted).astype(F32).astype(BF16)

    def add_part(which, e, part):
        back = dot(order_back(e), part).reshape(n_ex, per_peer, width)
        x_send[which] = (x_send[which].astype(F32) + back).astype(BF16)

    def send_back(which):
        loop(1, n_ex, lambda i: y_copy(which, i).start())
        y_got[which, my_ex] = x_send[which, my_ex]

    def one_expert(e):
        c = 3 * e
        more = e < members - 1
        assemble(c, w_gate, in_blocks, hid_blocks)

        @pl.when(e > 0)
        def _():
            pass_on(c - 2)


        @pl.when(e == 0)
        def _():
            loop(1, n_ex, lambda i: x_copy(0, i).wait_recv())

        rows[...] = dot(order(e), x_got[0].reshape(all_rows, width)).astype(BF16)
        rows_t[pl.ds(0, in_blocks)] = turned(rows[...])
        pre_gate[...] = dot(rows[...], w_gate[...])
        gating = sigma(
            jnp.sum(rows[...].astype(F32) * router[e], axis=1, keepdims=True)
        )
        assemble(c + 1, w_up, in_blocks, hid_blocks)
        pl.when(more)(lambda: forward(c + 3))
        pre_up[...] = dot(rows[...], w_up[...])
        gate = pre_gate[...]
        hidden[...] = (gate * sigma(gate) * pre_up[...]).astype(BF16)

        @pl.when(e == 0)
        def _():
            loop(1, n_ex, lambda i: x_copy(1, i).wait_recv())

            def sent(i):
                for which in range(2):
                    x_copy(which, i).wait_send()

            loop(1, n_ex, sent)
            x_send[...] = jnp.zeros(x_send.shape, BF16)

        grad_rows = dot(order(e), x_got[1].reshape(all_rows, width))
        scaled[...] = (gating * grad_rows).astype(BF16)
        hidden_t[pl.ds(0, hid_blocks)] = turned(hidden[...])
        scaled_t[...] = turned(scaled[...])
        assemble(c + 2, w_down, hid_blocks, in_blocks)
        extract(c + 2, hidden_t, scaled_t)
        pl.when(more)(lambda: forward(c + 4))
        outs[...] = dot(hidden[...], w_down[...])
        add_part(0, e, (gating * outs[...]).astype(BF16))
        grad_rows = dot(order(e), x_got[1].reshape(all_rows, width))
        logit = (
            jnp.sum(grad_rows * outs[...], axis=1, keepdims=True) * gating * (1.0 - gating)
        )
        r_send[e] = jnp.sum(rows[...].astype(F32) * logit, axis=0, keepdims=True)

        @pl.when(e == members - 1)
        def _():
            for i in range(1, n_dp):
                r_copy(i).start()
            send_back(0)

        pl.when(more)(lambda: forward(c + 5))
        hidden_grad = dot(scaled[...], w_down[...], ((1,), (1,)))
        gate = pre_gate[...]
        sig = sigma(gate)
        gate_grad = hidden_grad * pre_up[...] * sig * (1.0 + gate * (1.0 - sig))
        up_grad = hidden_grad * gate * sig
        pre_gate[...] = gate_grad
        pre_up[...] = up_grad
        inner_t[...] = turned(pre_gate[...].astype(BF16))
        extract(c, rows_t, inner_t)
        pass_on(c + 2)
        inner_t[...] = turned(pre_up[...].astype(BF16))
        extract(c + 1, rows_t, inner_t)
        pass_on(c)
        part = dot(pre_gate[...].astype(BF16), w_gate[...], ((1,), (1,)))
        part = part + dot(pre_up[...].astype(BF16), w_up[...], ((1,), (1,)))
        add_part(1, e, (part + logit * router[e]).astype(BF16))

    loop(0, members, one_expert)
    send_back(1)
    pass_on(3 * members - 2)

    def finish(c):
        for k in range(2, 6):
            g_copy(c, k).wait_recv()

        def add(q):
            total = own[c, q].astype(F32)
            for k in range(2):
                total = total + got[c, k, q].astype(F32)
            tiles[pl.ds(pl.multiple_of(q * BS, BS), BS), :] = total

        loop(0, pairs, add, 4)

        def separate(q):
            even = tiles[pl.ds(q * BS, half, stride=2), :]
            odd = tiles[pl.ds(q * BS + 1, half, stride=2), :]
            paired[pl.ds(pl.multiple_of(q * half, half), half), :] = jnp.where(
                half_low, even, pltpu.roll(odd, BS, 1)
            )
            paired[pl.ds(pl.multiple_of((q + pairs) * half, half), half), :] = jnp.where(
                half_low, pltpu.roll(even, BS, 1), odd
            )

        loop(0, pairs, separate, 4)
        score = jnp.zeros((2 * pairs, LANES), F32)
        for j in range(half):
            part = paired[pl.ds(j, 2 * pairs, stride=half), :]
            master = masters[c, :, j * LANES : (j + 1) * LANES]
            master_new[c, :, j * LANES : (j + 1) * LANES] = master - LEARN_RATE * part
            score = score + master * part
        score_sum[c] = jnp.sum(score, axis=1, keepdims=True)

    def finish_expert(e):
        for m in (2, 0, 1):
            finish(3 * e + m)

    loop(0, members - 1, finish_expert)
    placed = (
        lax.broadcasted_iota(jnp.int32, (tokens.shape[0], all_rows), 0) == picks_row[...]
    ).astype(F32).astype(BF16)
    loop(1, n_ex, lambda i: y_copy(0, i).wait_recv())
    layer_out[...] = dot(placed, y_got[0].reshape(all_rows, width)).astype(BF16)
    loop(1, n_ex, lambda i: y_copy(1, i).wait_recv())
    input_grad[...] = dot(placed, y_got[1].reshape(all_rows, width)).astype(BF16)

    for i in range(1, n_dp):
        r_copy(i).wait()
    share = width // n_dp
    mine = pl.ds(pl.multiple_of(my_dp * share, share), share)
    for e in range(members):
        router_total = r_send[e, :, mine]
        for i in range(1, n_dp):
            router_total = router_total + r_got[i - 1, e, :, mine]
        router_out[e] = router_total

    finish_expert(members - 1)

    def drain_weights(c):
        for k in range(6):
            g_copy(c, k).wait_send()

    loop(0, 3 * members, drain_weights)

    def drain_rows(i):
        for which in range(2):
            y_copy(which, i).wait_send()

    loop(1, n_ex, drain_rows)


def body(tokens, out_grad, token_picks, router, kept_blocks, masters, scores):
    members = kept_blocks.shape[0]
    slots = kept_blocks.shape[2]
    n_ex = lax.axis_size("expert")
    n_dp = lax.axis_size("dp")
    cap = token_picks.shape[2]
    width = tokens.shape[1]
    in_blocks = width // BS
    hid_blocks = FF // BS
    blocks = in_blocks * hid_blocks
    local = masters.shape[2]
    pairs = local // 2
    total_pairs = pairs * n_dp
    chunks = 3 * members
    all_rows = n_ex * members * cap
    expert_rows = n_ex * cap

    kept = kept_blocks.reshape(chunks, slots)
    numbers = jnp.arange(blocks, dtype=jnp.int32)
    hits = kept[:, None, :] == numbers[None, :, None]
    slot_of = jnp.sum(
        jnp.where(hits, jnp.arange(slots, dtype=jnp.int32) + 1, 0), axis=2
    ) - 1
    within = slot_of % local
    flipped = (within // pairs) != (numbers % 2)[None, :]
    place = (slot_of // local) * pairs + within % pairs + jnp.where(flipped, total_pairs, 0)
    place = jnp.where(slot_of >= 0, place, 2 * total_pairs).reshape(-1)

    col_counts = jnp.array([hid_blocks, hid_blocks, in_blocks] * members, jnp.int32)[:, None]
    empty = jnp.array([in_blocks, in_blocks, hid_blocks] * members, jnp.int32)[:, None] * BS
    code = (kept // col_counts) * BS + kept % col_counts
    code = jnp.where(kept < blocks, code, empty).reshape(-1)

    picks = token_picks[0].reshape(-1)
    router_rows = router.T.astype(F32).reshape(members, 1, width)

    vmem = pl.BlockSpec(memory_space=pltpu.VMEM)
    smem = pl.BlockSpec(memory_space=pltpu.SMEM)
    dma = pltpu.SemaphoreType.DMA
    layer_out, input_grad, master_new, score_sum, router_grad = pl.pallas_call(
        functools.partial(kernel, (n_dp, n_ex, members, cap)),
        out_shape=(
            jax.ShapeDtypeStruct(tokens.shape, BF16),
            jax.ShapeDtypeStruct(tokens.shape, BF16),
            jax.ShapeDtypeStruct((chunks, local, BS * BS), F32),
            jax.ShapeDtypeStruct((chunks, local, 1), F32),
            jax.ShapeDtypeStruct((members, 1, width // n_dp), F32),
        ),
        in_specs=[smem, smem] + [vmem] * 6,
        out_specs=[vmem] * 5,
        scratch_shapes=[
            pltpu.VMEM((chunks, pairs, BS, LANES), BF16),
            pltpu.VMEM((local * BS // 2, LANES), F32),
            pltpu.VMEM((pairs * BS, LANES), F32),
            pltpu.VMEM((chunks, n_dp - 1, pairs, BS, LANES), BF16),
            pltpu.VMEM((2 * total_pairs + 1, BS, LANES), BF16),
            pltpu.VMEM((width, FF), BF16),
            pltpu.VMEM((width, FF), BF16),
            pltpu.VMEM((FF, width), BF16),
            pltpu.VMEM((in_blocks + 1, BS, expert_rows), BF16),
            pltpu.VMEM((hid_blocks + 1, BS, expert_rows), BF16),
            pltpu.VMEM((in_blocks, BS, expert_rows), BF16),
            pltpu.VMEM((hid_blocks, BS, expert_rows), BF16),
            pltpu.VMEM((chunks, 2, pairs, BS, LANES), BF16),
            pltpu.VMEM((chunks, 2, pairs // 2, BS, LANES), BF16),
            pltpu.VMEM((2, n_ex, members * cap, width), BF16),
            pltpu.VMEM((2, n_ex, members * cap, width), BF16),
            pltpu.VMEM((2, n_ex, members * cap, width), BF16),
            pltpu.VMEM((expert_rows, width), BF16),
            pltpu.VMEM((expert_rows, width), BF16),
            pltpu.VMEM((expert_rows, FF), BF16),
            pltpu.VMEM((expert_rows, FF), F32),
            pltpu.VMEM((expert_rows, FF), F32),
            pltpu.VMEM((expert_rows, width), F32),
            pltpu.VMEM((members, 1, width), F32),
            pltpu.VMEM((n_dp - 1, members, 1, width), F32),
            dma((chunks, 4)),
            dma((chunks, 4)),
            dma((chunks, 6)),
            dma((chunks, 6)),
            dma((2, n_ex - 1)),
            dma((2, n_ex - 1)),
            dma((2, n_ex - 1)),
            dma((2, n_ex - 1)),
            dma((n_dp - 1,)),
            dma((n_dp - 1,)),
        ],
        compiler_params=pltpu.CompilerParams(
            collective_id=0, has_side_effects=True, vmem_limit_bytes=62 * 1024 * 1024
        ),
    )(
        place,
        code,
        picks.reshape(all_rows, 1),
        picks.reshape(1, all_rows),
        tokens,
        out_grad,
        router_rows,
        masters.reshape(chunks, local, BS * BS),
    )

    master_new = master_new.reshape(masters.shape)
    score_new = scores - SCORE_RATE * score_sum.reshape(scores.shape)
    return layer_out, input_grad, master_new, score_new, router_grad.reshape(members, -1).T


def solution(mesh):
    return jax.shard_map(
        body,
        mesh=mesh,
        in_specs=(
            P(("dp", "expert"), None),
            P(("dp", "expert"), None),
            P(("dp", "expert"), None, None),
            P(None, "expert"),
            P("expert", None, None),
            P("expert", None, "dp", None),
            P("expert", None, "dp"),
        ),
        out_specs=(
            P(("dp", "expert"), None),
            P(("dp", "expert"), None),
            P("expert", None, "dp", None),
            P("expert", None, "dp"),
            P("dp", "expert"),
        ),
        check_vma=False,
    )
```

```python
import functools

import jax
import jax.numpy as jnp
from jax import lax
from jax.experimental import pallas as pl
from jax.experimental.pallas import tpu as pltpu
from jax.sharding import PartitionSpec as P

FF = 768
BS = 64
LANES = 2 * BS

LEARN_RATE = 0.005
SCORE_RATE = 0.05

F32 = jnp.float32
BF16 = jnp.bfloat16


def dot(a, b, dims=((1,), (0,))):
    return lax.dot_general(a, b, (dims, ((), ())), preferred_element_type=F32)


def sigma(v):
    return 1.0 / (1.0 + jnp.exp(-v))


def kernel(
    sizes,
    place_ref,
    pick_ref,
    picks_col,
    picks_row,
    tokens,
    out_grad,
    router,
    masters,
    layer_out,
    input_grad,
    master_new,
    score_sum,
    router_out,
    own,
    paired,
    tiles,
    held,
    stage,
    w_gate,
    w_up,
    w_down,
    rows_t,
    hidden_t,
    scaled_t,
    inner_t,
    got,
    relay,
    x_send,
    x_got,
    y_got,
    rows,
    scaled,
    hidden,
    pre_gate,
    pre_up,
    outs,
    r_send,
    r_got,
    w_ssem,
    w_rsem,
    g_ssem,
    g_rsem,
    x_ssem,
    x_rsem,
    y_ssem,
    y_rsem,
    r_ssem,
    r_rsem,
):
    n_dp, n_ex, members, cap = sizes
    width = tokens.shape[1]
    in_blocks = width // BS
    hid_blocks = FF // BS
    blocks = in_blocks * hid_blocks
    pairs = masters.shape[1] // 2
    total_pairs = pairs * n_dp
    slots = 2 * total_pairs
    per_peer = members * cap
    all_rows = n_ex * per_peer
    expert_rows = n_ex * cap
    my_dp = lax.axis_index("dp")
    my_ex = lax.axis_index("expert")

    def ahead(i):
        return lax.rem(my_dp + i, n_dp)

    near_a = my_dp + 1 - 2 * (my_dp % 2)
    near_b = my_dp + 2 - 4 * (my_dp // 2)
    across = n_dp - 1 - my_dp

    def peer(i):
        return lax.rem(my_ex + i, n_ex)

    def loop(lo, hi, fn, unroll=1):
        def step(i, carry):
            fn(i)
            return carry

        lax.fori_loop(lo, hi, step, 0, unroll=unroll)

    barrier = pltpu.get_barrier_semaphore()
    for i in range(1, n_dp):
        pl.semaphore_signal(
            barrier, inc=1, device_id={"dp": ahead(i)}, device_id_type=pl.DeviceIdType.MESH
        )
    loop(
        1,
        n_ex,
        lambda i: pl.semaphore_signal(
            barrier, inc=1, device_id={"expert": peer(i)}, device_id_type=pl.DeviceIdType.MESH
        ),
    )

    chosen = (
        lax.broadcasted_iota(jnp.int32, (all_rows, tokens.shape[0]), 1) == picks_col[...]
    ).astype(F32).astype(BF16)
    x_send[0] = dot(chosen, tokens[...]).astype(BF16).reshape(n_ex, per_peer, width)
    x_send[1] = dot(chosen, out_grad[...]).astype(BF16).reshape(n_ex, per_peer, width)
    stage[2 * total_pairs] = jnp.zeros((BS, LANES), BF16)
    rows_t[in_blocks] = jnp.zeros((BS, expert_rows), BF16)
    hidden_t[hid_blocks] = jnp.zeros((BS, expert_rows), BF16)
    same = (
        lax.broadcasted_iota(jnp.int32, (expert_rows, expert_rows), 0)
        == lax.broadcasted_iota(jnp.int32, (expert_rows, expert_rows), 1)
    ).astype(F32).astype(BF16)

    def turned(value):
        return dot(value, same, ((0,), (0,))).astype(BF16).reshape(-1, BS, expert_rows)


    half_low = lax.broadcasted_iota(jnp.int32, (BS // 2, LANES), 1) < BS
    half = BS // 2

    def pack(c):
        for j in range(half):
            paired[pl.ds(j, 2 * pairs, stride=half), :] = masters[c, :, j * LANES : (j + 1) * LANES]

        def interleave(q):
            first = paired[pl.ds(pl.multiple_of(q * half, half), half), :]
            second = paired[pl.ds(pl.multiple_of((q + pairs) * half, half), half), :]
            tiles[pl.ds(q * BS, half, stride=2), :] = jnp.where(
                half_low, first, pltpu.roll(second, BS, 1)
            )
            tiles[pl.ds(q * BS + 1, half, stride=2), :] = jnp.where(
                half_low, pltpu.roll(first, BS, 1), second
            )

        loop(0, pairs, interleave, 8)

        def narrow(q):
            own[c, q] = tiles[pl.ds(pl.multiple_of(q * BS, BS), BS), :].astype(BF16)

        loop(0, pairs, narrow, 8)

    pack(0)
    pl.semaphore_wait(barrier, n_dp - 1 + n_ex - 1)

    def x_copy(which, i):
        return pltpu.make_async_remote_copy(
            src_ref=x_send.at[which, peer(i)],
            dst_ref=x_got.at[which, my_ex],
            send_sem=x_ssem.at[which, i - 1],
            recv_sem=x_rsem.at[which, i - 1],
            device_id={"expert": peer(i)},
            device_id_type=pl.DeviceIdType.MESH,
        )

    def y_copy(which, i):
        return pltpu.make_async_remote_copy(
            src_ref=x_send.at[which, peer(i)],
            dst_ref=y_got.at[which, my_ex],
            send_sem=y_ssem.at[which, i - 1],
            recv_sem=y_rsem.at[which, i - 1],
            device_id={"expert": peer(i)},
            device_id_type=pl.DeviceIdType.MESH,
        )

    first_half = pl.ds(0, pairs // 2)
    last_half = pl.ds(pairs // 2, pairs // 2)

    def dp_copy(src, dst, send_sem, recv_sem, device):
        return pltpu.make_async_remote_copy(
            src_ref=src,
            dst_ref=dst,
            send_sem=send_sem,
            recv_sem=recv_sem,
            device_id={"dp": device},
            device_id_type=pl.DeviceIdType.MESH,
        )

    def w_copy(c, k):
        src, dst, device = (
            (own.at[c], held.at[c, 0], near_a),
            (own.at[c], held.at[c, 1], near_b),
            (held.at[c, 0, first_half], held.at[c, 2, first_half], near_b),
            (held.at[c, 1, last_half], held.at[c, 2, last_half], near_a),
        )[k]
        return dp_copy(src, dst, w_ssem.at[c, k], w_rsem.at[c, k], device)

    def g_copy(c, k):
        src, dst, device = (
            (held.at[c, 2, first_half], relay.at[c, 0], near_a),
            (held.at[c, 2, last_half], relay.at[c, 1], near_b),
            (held.at[c, 0, first_half], got.at[c, 0, first_half], near_a),
            (held.at[c, 1, last_half], got.at[c, 1, last_half], near_b),
            (held.at[c, 0, last_half], got.at[c, 0, last_half], near_a),
            (held.at[c, 1, first_half], got.at[c, 1, first_half], near_b),
        )[k]
        return dp_copy(src, dst, g_ssem.at[c, k], g_rsem.at[c, k], device)

    def r_copy(i):
        return pltpu.make_async_remote_copy(
            src_ref=r_send,
            dst_ref=r_got.at[i - 1],
            send_sem=r_ssem.at[i - 1],
            recv_sem=r_rsem.at[i - 1],
            device_id={"dp": ahead(i)},
            device_id_type=pl.DeviceIdType.MESH,
        )

    def send_weights(c):
        w_copy(c, 0).start()
        w_copy(c, 1).start()

    def forward(c):
        for k in (0, 1):
            w_copy(c, k).wait_recv()
        for k in (2, 3):
            w_copy(c, k).start()

    send_weights(0)
    loop(1, n_ex, lambda i: x_copy(0, i).start())
    pack(1)
    send_weights(1)
    loop(1, n_ex, lambda i: x_copy(1, i).start())
    for which in range(2):
        x_got[which, my_ex] = x_send[which, my_ex]
    loop(2, 3 * members, pack)
    forward(0)
    forward(1)
    send_weights(2)

    low = lax.broadcasted_iota(jnp.int32, (BS, LANES), 1) < BS

    def load_stage(c):
        def put(base, tile):
            stage[base] = tile
            stage[total_pairs + base] = pltpu.roll(tile.astype(F32), BS, 1).astype(BF16)

        loop(0, pairs, lambda q: put(my_dp * pairs + q, own[c, q]), 8)
        for k, shard in enumerate((near_a, near_b)):
            loop(0, pairs, lambda q: put(shard * pairs + q, held[c, k, q]), 8)
        w_copy(c, 2).wait_recv()
        w_copy(c, 3).wait_recv()
        loop(0, pairs, lambda q: put(across * pairs + q, held[c, 2, q]), 8)

    def assemble(c, target, row_blocks, col_blocks):
        load_stage(c)

        def one_row(r):
            start = pl.multiple_of(r * BS, BS)
            for k in range(col_blocks // 2):
                at = c * blocks + r * col_blocks + 2 * k
                tile = jnp.where(low, stage[place_ref[at]], stage[place_ref[at + 1]])
                target[pl.ds(start, BS), k * LANES : (k + 1) * LANES] = tile

        loop(0, row_blocks, one_row, 4)

    def extract(c, left, right):
        def slot(at):
            code = pick_ref[at]
            return left[code // BS], right[code % BS]

        def tile(d, q):
            at = c * slots + d * 2 * pairs + q
            left0, right0 = slot(at)
            left1, right1 = slot(at + pairs)
            both = dot(
                jnp.concatenate([left0, left1], axis=0),
                jnp.concatenate([right0, right1], axis=0),
                ((1,), (1,)),
            )
            return jnp.where(low, both[:BS], both[BS:])

        for k in range(4):
            w_copy(c, k).wait_send()
        for k, shard in ((2, across), (0, near_a), (1, near_b)):

            def fill(q):
                held[c, k, q] = tile(shard, q).astype(BF16)

            loop(0, pairs, fill, 8)
            for g in ((2,), (3,), (0, 1))[k]:
                g_copy(c, g).start()

        def keep(q):
            own[c, q] = tile(my_dp, q).astype(BF16)

        loop(0, pairs, keep, 8)

    def pass_on(c):
        g_copy(c, 0).wait_recv()
        g_copy(c, 1).wait_recv()

        def add(q):
            later = q + pairs // 2
            held[c, 0, later] = (held[c, 0, later].astype(F32) + relay[c, 1, q].astype(F32)).astype(BF16)
            held[c, 1, q] = (held[c, 1, q].astype(F32) + relay[c, 0, q].astype(F32)).astype(BF16)

        loop(0, pairs // 2, add, 4)
        g_copy(c, 4).start()
        g_copy(c, 5).start()

    def order(e):
        at = lax.broadcasted_iota(jnp.int32, (expert_rows, all_rows), 0)
        col = lax.broadcasted_iota(jnp.int32, (expert_rows, all_rows), 1)
        wanted = (at // cap) * per_peer + e * cap + at % cap
        return (col == wanted).astype(F32).astype(BF16)

    def order_back(e):
        col = lax.broadcasted_iota(jnp.int32, (all_rows, expert_rows), 1)
        at = lax.broadcasted_iota(jnp.int32, (all_rows, expert_rows), 0)
        wanted = (col // cap) * per_peer + e * cap + col % cap
        return (at == wanted).astype(F32).astype(BF16)

    def add_part(which, e, part):
        back = dot(order_back(e), part).reshape(n_ex, per_peer, width)
        x_send[which] = (x_send[which].astype(F32) + back).astype(BF16)

    def send_back(which):
        loop(1, n_ex, lambda i: y_copy(which, i).start())
        y_got[which, my_ex] = x_send[which, my_ex]

    def one_expert(e):
        c = 3 * e
        more = e < members - 1

        @pl.when(e == 0)
        def _():
            loop(1, n_ex, lambda i: x_copy(0, i).wait_recv())

        rows[...] = dot(order(e), x_got[0].reshape(all_rows, width)).astype(BF16)
        rows_t[pl.ds(0, in_blocks)] = turned(rows[...])
        gating = sigma(
            jnp.sum(rows[...].astype(F32) * router[e], axis=1, keepdims=True)
        )
        assemble(c, w_gate, in_blocks, hid_blocks)

        @pl.when(e == 0)
        def _():
            forward(2)
            loop(3, 3 * members, send_weights)

        @pl.when(e > 0)
        def _():
            pass_on(c - 2)

        pre_gate[...] = dot(rows[...], w_gate[...])
        assemble(c + 1, w_up, in_blocks, hid_blocks)
        pre_up[...] = dot(rows[...], w_up[...])
        gate = pre_gate[...]
        hidden[...] = (gate * sigma(gate) * pre_up[...]).astype(BF16)

        @pl.when(e == 0)
        def _():
            loop(1, n_ex, lambda i: x_copy(1, i).wait_recv())

            def sent(i):
                for which in range(2):
                    x_copy(which, i).wait_send()

            loop(1, n_ex, sent)
            x_send[...] = jnp.zeros(x_send.shape, BF16)

        grad_rows = dot(order(e), x_got[1].reshape(all_rows, width))
        scaled[...] = (gating * grad_rows).astype(BF16)
        hidden_t[pl.ds(0, hid_blocks)] = turned(hidden[...])
        scaled_t[...] = turned(scaled[...])
        assemble(c + 2, w_down, hid_blocks, in_blocks)
        extract(c + 2, hidden_t, scaled_t)
        pl.when(more)(lambda: forward(c + 3))
        outs[...] = dot(hidden[...], w_down[...])
        add_part(0, e, (gating * outs[...]).astype(BF16))
        grad_rows = dot(order(e), x_got[1].reshape(all_rows, width))
        logit = (
            jnp.sum(grad_rows * outs[...], axis=1, keepdims=True) * gating * (1.0 - gating)
        )
        r_send[e] = jnp.sum(rows[...].astype(F32) * logit, axis=0, keepdims=True)

        @pl.when(e == members - 1)
        def _():
            for i in range(1, n_dp):
                r_copy(i).start()
            send_back(0)

        pl.when(more)(lambda: forward(c + 4))
        hidden_grad = dot(scaled[...], w_down[...], ((1,), (1,)))
        pl.when(more)(lambda: forward(c + 5))
        gate = pre_gate[...]
        sig = sigma(gate)
        gate_grad = hidden_grad * pre_up[...] * sig * (1.0 + gate * (1.0 - sig))
        up_grad = hidden_grad * gate * sig
        pre_gate[...] = gate_grad
        pre_up[...] = up_grad
        inner_t[...] = turned(pre_gate[...].astype(BF16))
        extract(c, rows_t, inner_t)
        pass_on(c + 2)
        inner_t[...] = turned(pre_up[...].astype(BF16))
        extract(c + 1, rows_t, inner_t)
        pass_on(c)
        part = dot(pre_gate[...].astype(BF16), w_gate[...], ((1,), (1,)))
        part = part + dot(pre_up[...].astype(BF16), w_up[...], ((1,), (1,)))
        add_part(1, e, (part + logit * router[e]).astype(BF16))

    loop(0, members, one_expert)
    send_back(1)
    pass_on(3 * members - 2)

    def finish(c):
        for k in range(2, 6):
            g_copy(c, k).wait_recv()

        def add(q):
            total = own[c, q].astype(F32)
            for k in range(2):
                total = total + got[c, k, q].astype(F32)
            tiles[pl.ds(pl.multiple_of(q * BS, BS), BS), :] = total

        loop(0, pairs, add, 4)

        def separate(q):
            even = tiles[pl.ds(q * BS, half, stride=2), :]
            odd = tiles[pl.ds(q * BS + 1, half, stride=2), :]
            paired[pl.ds(pl.multiple_of(q * half, half), half), :] = jnp.where(
                half_low, even, pltpu.roll(odd, BS, 1)
            )
            paired[pl.ds(pl.multiple_of((q + pairs) * half, half), half), :] = jnp.where(
                half_low, pltpu.roll(even, BS, 1), odd
            )

        loop(0, pairs, separate, 8)
        score = jnp.zeros((2 * pairs, LANES), F32)
        for j in range(half):
            part = paired[pl.ds(j, 2 * pairs, stride=half), :]
            master = masters[c, :, j * LANES : (j + 1) * LANES]
            master_new[c, :, j * LANES : (j + 1) * LANES] = master - LEARN_RATE * part
            score = score + master * part
        score_sum[c] = jnp.sum(score, axis=1, keepdims=True)

    def finish_expert(e):
        for m in (2, 0, 1):
            finish(3 * e + m)

    loop(0, members - 1, finish_expert)
    placed = (
        lax.broadcasted_iota(jnp.int32, (tokens.shape[0], all_rows), 0) == picks_row[...]
    ).astype(F32).astype(BF16)
    loop(1, n_ex, lambda i: y_copy(0, i).wait_recv())
    layer_out[...] = dot(placed, y_got[0].reshape(all_rows, width)).astype(BF16)
    loop(1, n_ex, lambda i: y_copy(1, i).wait_recv())
    input_grad[...] = dot(placed, y_got[1].reshape(all_rows, width)).astype(BF16)

    for i in range(1, n_dp):
        r_copy(i).wait()
    share = width // n_dp
    mine = pl.ds(pl.multiple_of(my_dp * share, share), share)
    for e in range(members):
        router_total = r_send[e, :, mine]
        for i in range(1, n_dp):
            router_total = router_total + r_got[i - 1, e, :, mine]
        router_out[e] = router_total

    finish_expert(members - 1)

    def drain_weights(c):
        for k in range(6):
            g_copy(c, k).wait_send()

    loop(0, 3 * members, drain_weights)

    def drain_rows(i):
        for which in range(2):
            y_copy(which, i).wait_send()

    loop(1, n_ex, drain_rows)


def body(tokens, out_grad, token_picks, router, kept_blocks, masters, scores):
    members = kept_blocks.shape[0]
    slots = kept_blocks.shape[2]
    n_ex = lax.axis_size("expert")
    n_dp = lax.axis_size("dp")
    cap = token_picks.shape[2]
    width = tokens.shape[1]
    in_blocks = width // BS
    hid_blocks = FF // BS
    blocks = in_blocks * hid_blocks
    local = masters.shape[2]
    pairs = local // 2
    total_pairs = pairs * n_dp
    chunks = 3 * members
    all_rows = n_ex * members * cap
    expert_rows = n_ex * cap

    kept = kept_blocks.reshape(chunks, slots)
    numbers = jnp.arange(blocks, dtype=jnp.int32)
    hits = kept[:, None, :] == numbers[None, :, None]
    slot_of = jnp.sum(
        jnp.where(hits, jnp.arange(slots, dtype=jnp.int32) + 1, 0), axis=2
    ) - 1
    within = slot_of % local
    flipped = (within // pairs) != (numbers % 2)[None, :]
    place = (slot_of // local) * pairs + within % pairs + jnp.where(flipped, total_pairs, 0)
    place = jnp.where(slot_of >= 0, place, 2 * total_pairs).reshape(-1)

    col_counts = jnp.array([hid_blocks, hid_blocks, in_blocks] * members, jnp.int32)[:, None]
    empty = jnp.array([in_blocks, in_blocks, hid_blocks] * members, jnp.int32)[:, None] * BS
    code = (kept // col_counts) * BS + kept % col_counts
    code = jnp.where(kept < blocks, code, empty).reshape(-1)

    picks = token_picks[0].reshape(-1)
    router_rows = router.T.astype(F32).reshape(members, 1, width)

    vmem = pl.BlockSpec(memory_space=pltpu.VMEM)
    smem = pl.BlockSpec(memory_space=pltpu.SMEM)
    dma = pltpu.SemaphoreType.DMA
    layer_out, input_grad, master_new, score_sum, router_grad = pl.pallas_call(
        functools.partial(kernel, (n_dp, n_ex, members, cap)),
        out_shape=(
            jax.ShapeDtypeStruct(tokens.shape, BF16),
            jax.ShapeDtypeStruct(tokens.shape, BF16),
            jax.ShapeDtypeStruct((chunks, local, BS * BS), F32),
            jax.ShapeDtypeStruct((chunks, local, 1), F32),
            jax.ShapeDtypeStruct((members, 1, width // n_dp), F32),
        ),
        in_specs=[smem, smem] + [vmem] * 6,
        out_specs=[vmem] * 5,
        scratch_shapes=[
            pltpu.VMEM((chunks, pairs, BS, LANES), BF16),
            pltpu.VMEM((local * BS // 2, LANES), F32),
            pltpu.VMEM((pairs * BS, LANES), F32),
            pltpu.VMEM((chunks, n_dp - 1, pairs, BS, LANES), BF16),
            pltpu.VMEM((2 * total_pairs + 1, BS, LANES), BF16),
            pltpu.VMEM((width, FF), BF16),
            pltpu.VMEM((width, FF), BF16),
            pltpu.VMEM((FF, width), BF16),
            pltpu.VMEM((in_blocks + 1, BS, expert_rows), BF16),
            pltpu.VMEM((hid_blocks + 1, BS, expert_rows), BF16),
            pltpu.VMEM((in_blocks, BS, expert_rows), BF16),
            pltpu.VMEM((hid_blocks, BS, expert_rows), BF16),
            pltpu.VMEM((chunks, 2, pairs, BS, LANES), BF16),
            pltpu.VMEM((chunks, 2, pairs // 2, BS, LANES), BF16),
            pltpu.VMEM((2, n_ex, members * cap, width), BF16),
            pltpu.VMEM((2, n_ex, members * cap, width), BF16),
            pltpu.VMEM((2, n_ex, members * cap, width), BF16),
            pltpu.VMEM((expert_rows, width), BF16),
            pltpu.VMEM((expert_rows, width), BF16),
            pltpu.VMEM((expert_rows, FF), BF16),
            pltpu.VMEM((expert_rows, FF), F32),
            pltpu.VMEM((expert_rows, FF), F32),
            pltpu.VMEM((expert_rows, width), F32),
            pltpu.VMEM((members, 1, width), F32),
            pltpu.VMEM((n_dp - 1, members, 1, width), F32),
            dma((chunks, 4)),
            dma((chunks, 4)),
            dma((chunks, 6)),
            dma((chunks, 6)),
            dma((2, n_ex - 1)),
            dma((2, n_ex - 1)),
            dma((2, n_ex - 1)),
            dma((2, n_ex - 1)),
            dma((n_dp - 1,)),
            dma((n_dp - 1,)),
        ],
        compiler_params=pltpu.CompilerParams(
            collective_id=0, has_side_effects=True, vmem_limit_bytes=62 * 1024 * 1024
        ),
    )(
        place,
        code,
        picks.reshape(all_rows, 1),
        picks.reshape(1, all_rows),
        tokens,
        out_grad,
        router_rows,
        masters.reshape(chunks, local, BS * BS),
    )

    master_new = master_new.reshape(masters.shape)
    score_new = scores - SCORE_RATE * score_sum.reshape(scores.shape)
    return layer_out, input_grad, master_new, score_new, router_grad.reshape(members, -1).T


def solution(mesh):
    return jax.shard_map(
        body,
        mesh=mesh,
        in_specs=(
            P(("dp", "expert"), None),
            P(("dp", "expert"), None),
            P(("dp", "expert"), None, None),
            P(None, "expert"),
            P("expert", None, None),
            P("expert", None, "dp", None),
            P("expert", None, "dp"),
        ),
        out_specs=(
            P(("dp", "expert"), None),
            P(("dp", "expert"), None),
            P("expert", None, "dp", None),
            P("expert", None, "dp"),
            P("dp", "expert"),
        ),
        check_vma=False,
    )
```

```python
import functools

import jax
import jax.numpy as jnp
from jax import lax
from jax.experimental import pallas as pl
from jax.experimental.pallas import tpu as pltpu
from jax.sharding import PartitionSpec as P

FF = 768
BS = 64
LANES = 2 * BS

LEARN_RATE = 0.005
SCORE_RATE = 0.05

F32 = jnp.float32
BF16 = jnp.bfloat16


def dot(a, b, dims=((1,), (0,))):
    return lax.dot_general(a, b, (dims, ((), ())), preferred_element_type=F32)


def sigma(v):
    return 1.0 / (1.0 + jnp.exp(-v))


def kernel(
    sizes,
    place_ref,
    pick_ref,
    picks_col,
    picks_row,
    tokens,
    out_grad,
    router,
    masters,
    layer_out,
    input_grad,
    master_new,
    score_sum,
    router_out,
    own,
    paired,
    tiles,
    held,
    stage,
    w_gate,
    w_up,
    w_down,
    rows_t,
    hidden_t,
    scaled_t,
    inner_t,
    got,
    relay,
    x_send,
    x_got,
    y_got,
    rows,
    scaled,
    hidden,
    pre_gate,
    pre_up,
    outs,
    r_send,
    r_got,
    w_ssem,
    w_rsem,
    g_ssem,
    g_rsem,
    x_ssem,
    x_rsem,
    y_ssem,
    y_rsem,
    r_ssem,
    r_rsem,
):
    n_dp, n_ex, members, cap = sizes
    width = tokens.shape[1]
    in_blocks = width // BS
    hid_blocks = FF // BS
    blocks = in_blocks * hid_blocks
    pairs = masters.shape[1] // 2
    total_pairs = pairs * n_dp
    slots = 2 * total_pairs
    per_peer = members * cap
    all_rows = n_ex * per_peer
    expert_rows = n_ex * cap
    my_dp = lax.axis_index("dp")
    my_ex = lax.axis_index("expert")

    def ahead(i):
        return lax.rem(my_dp + i, n_dp)

    near_a = my_dp + 1 - 2 * (my_dp % 2)
    near_b = my_dp + 2 - 4 * (my_dp // 2)
    across = n_dp - 1 - my_dp

    def peer(i):
        return lax.rem(my_ex + i, n_ex)

    def loop(lo, hi, fn, unroll=1):
        def step(i, carry):
            fn(i)
            return carry

        lax.fori_loop(lo, hi, step, 0, unroll=unroll)

    barrier = pltpu.get_barrier_semaphore()
    for i in range(1, n_dp):
        pl.semaphore_signal(
            barrier, inc=1, device_id={"dp": ahead(i)}, device_id_type=pl.DeviceIdType.MESH
        )
    loop(
        1,
        n_ex,
        lambda i: pl.semaphore_signal(
            barrier, inc=1, device_id={"expert": peer(i)}, device_id_type=pl.DeviceIdType.MESH
        ),
    )

    chosen = (
        lax.broadcasted_iota(jnp.int32, (all_rows, tokens.shape[0]), 1) == picks_col[...]
    ).astype(F32).astype(BF16)
    x_send[0] = dot(chosen, tokens[...]).astype(BF16).reshape(n_ex, per_peer, width)
    x_send[1] = dot(chosen, out_grad[...]).astype(BF16).reshape(n_ex, per_peer, width)
    stage[2 * total_pairs] = jnp.zeros((BS, LANES), BF16)
    rows_t[in_blocks] = jnp.zeros((BS, expert_rows), BF16)
    hidden_t[hid_blocks] = jnp.zeros((BS, expert_rows), BF16)
    same = (
        lax.broadcasted_iota(jnp.int32, (expert_rows, expert_rows), 0)
        == lax.broadcasted_iota(jnp.int32, (expert_rows, expert_rows), 1)
    ).astype(F32).astype(BF16)

    def turned(value):
        return dot(value, same, ((0,), (0,))).astype(BF16).reshape(-1, BS, expert_rows)


    half_low = lax.broadcasted_iota(jnp.int32, (BS // 2, LANES), 1) < BS
    half = BS // 2

    def pack(c):
        for j in range(half):
            paired[pl.ds(j, 2 * pairs, stride=half), :] = masters[c, :, j * LANES : (j + 1) * LANES]

        def interleave(q):
            first = paired[pl.ds(pl.multiple_of(q * half, half), half), :]
            second = paired[pl.ds(pl.multiple_of((q + pairs) * half, half), half), :]
            tiles[pl.ds(q * BS, half, stride=2), :] = jnp.where(
                half_low, first, pltpu.roll(second, BS, 1)
            )
            tiles[pl.ds(q * BS + 1, half, stride=2), :] = jnp.where(
                half_low, pltpu.roll(first, BS, 1), second
            )

        loop(0, pairs, interleave, 8)

        def narrow(q):
            own[c, q] = tiles[pl.ds(pl.multiple_of(q * BS, BS), BS), :].astype(BF16)

        loop(0, pairs, narrow, 8)

    pack(0)
    pl.semaphore_wait(barrier, n_dp - 1 + n_ex - 1)

    def x_copy(which, i):
        return pltpu.make_async_remote_copy(
            src_ref=x_send.at[which, peer(i)],
            dst_ref=x_got.at[which, my_ex],
            send_sem=x_ssem.at[which, i - 1],
            recv_sem=x_rsem.at[which, i - 1],
            device_id={"expert": peer(i)},
            device_id_type=pl.DeviceIdType.MESH,
        )

    def y_copy(which, i):
        return pltpu.make_async_remote_copy(
            src_ref=x_send.at[which, peer(i)],
            dst_ref=y_got.at[which, my_ex],
            send_sem=y_ssem.at[which, i - 1],
            recv_sem=y_rsem.at[which, i - 1],
            device_id={"expert": peer(i)},
            device_id_type=pl.DeviceIdType.MESH,
        )

    first_half = pl.ds(0, pairs // 2)
    last_half = pl.ds(pairs // 2, pairs // 2)

    def dp_copy(src, dst, send_sem, recv_sem, device):
        return pltpu.make_async_remote_copy(
            src_ref=src,
            dst_ref=dst,
            send_sem=send_sem,
            recv_sem=recv_sem,
            device_id={"dp": device},
            device_id_type=pl.DeviceIdType.MESH,
        )

    def w_copy(c, k):
        src, dst, device = (
            (own.at[c], held.at[c, 0], near_a),
            (own.at[c], held.at[c, 1], near_b),
            (held.at[c, 0, first_half], held.at[c, 2, first_half], near_b),
            (held.at[c, 1, last_half], held.at[c, 2, last_half], near_a),
        )[k]
        return dp_copy(src, dst, w_ssem.at[c, k], w_rsem.at[c, k], device)

    def g_copy(c, k):
        src, dst, device = (
            (held.at[c, 2, first_half], relay.at[c, 0], near_a),
            (held.at[c, 2, last_half], relay.at[c, 1], near_b),
            (held.at[c, 0, first_half], got.at[c, 0, first_half], near_a),
            (held.at[c, 1, last_half], got.at[c, 1, last_half], near_b),
            (held.at[c, 0, last_half], got.at[c, 0, last_half], near_a),
            (held.at[c, 1, first_half], got.at[c, 1, first_half], near_b),
        )[k]
        return dp_copy(src, dst, g_ssem.at[c, k], g_rsem.at[c, k], device)

    def r_copy(i):
        return pltpu.make_async_remote_copy(
            src_ref=r_send,
            dst_ref=r_got.at[i - 1],
            send_sem=r_ssem.at[i - 1],
            recv_sem=r_rsem.at[i - 1],
            device_id={"dp": ahead(i)},
            device_id_type=pl.DeviceIdType.MESH,
        )

    def send_weights(c):
        w_copy(c, 0).start()
        w_copy(c, 1).start()

    def forward(c):
        for k in (0, 1):
            w_copy(c, k).wait_recv()
        for k in (2, 3):
            w_copy(c, k).start()

    send_weights(0)
    loop(1, n_ex, lambda i: x_copy(0, i).start())
    pack(1)
    send_weights(1)
    loop(1, n_ex, lambda i: x_copy(1, i).start())
    for which in range(2):
        x_got[which, my_ex] = x_send[which, my_ex]
    loop(2, 3 * members, pack)
    forward(0)
    forward(1)
    send_weights(2)

    low = lax.broadcasted_iota(jnp.int32, (BS, LANES), 1) < BS

    def load_stage(c):
        def put(base, tile):
            stage[base] = tile
            stage[total_pairs + base] = pltpu.roll(tile.astype(F32), BS, 1).astype(BF16)

        loop(0, pairs, lambda q: put(my_dp * pairs + q, own[c, q]), 8)
        for k, shard in enumerate((near_a, near_b)):
            loop(0, pairs, lambda q: put(shard * pairs + q, held[c, k, q]), 8)
        w_copy(c, 2).wait_recv()
        w_copy(c, 3).wait_recv()
        loop(0, pairs, lambda q: put(across * pairs + q, held[c, 2, q]), 8)

    def assemble(c, target, row_blocks, col_blocks):
        load_stage(c)

        def one_row(r):
            start = pl.multiple_of(r * BS, BS)
            for k in range(col_blocks // 2):
                at = c * blocks + r * col_blocks + 2 * k
                tile = jnp.where(low, stage[place_ref[at]], stage[place_ref[at + 1]])
                target[pl.ds(start, BS), k * LANES : (k + 1) * LANES] = tile

        loop(0, row_blocks, one_row, 4)

    def extract(c, left, right):
        def slot(at):
            code = pick_ref[at]
            return left[code // BS], right[code % BS]

        def tile(d, q):
            at = c * slots + d * 2 * pairs + q
            left0, right0 = slot(at)
            left1, right1 = slot(at + pairs)
            both = dot(
                jnp.concatenate([left0, left1], axis=0),
                jnp.concatenate([right0, right1], axis=0),
                ((1,), (1,)),
            )
            return jnp.where(low, both[:BS], both[BS:])

        for k in range(4):
            w_copy(c, k).wait_send()
        for k, shard in ((2, across), (0, near_a), (1, near_b)):

            def fill(q):
                held[c, k, q] = tile(shard, q).astype(BF16)

            loop(0, pairs, fill, 8)
            for g in ((2,), (3,), (0, 1))[k]:
                g_copy(c, g).start()

        def keep(q):
            own[c, q] = tile(my_dp, q).astype(BF16)

        loop(0, pairs, keep, 8)

    def pass_on(c):
        g_copy(c, 0).wait_recv()
        g_copy(c, 1).wait_recv()

        def add(q):
            later = q + pairs // 2
            held[c, 0, later] = (held[c, 0, later].astype(F32) + relay[c, 1, q].astype(F32)).astype(BF16)
            held[c, 1, q] = (held[c, 1, q].astype(F32) + relay[c, 0, q].astype(F32)).astype(BF16)

        loop(0, pairs // 2, add, 4)
        g_copy(c, 4).start()
        g_copy(c, 5).start()

    def order(e):
        at = lax.broadcasted_iota(jnp.int32, (expert_rows, all_rows), 0)
        col = lax.broadcasted_iota(jnp.int32, (expert_rows, all_rows), 1)
        wanted = (at // cap) * per_peer + e * cap + at % cap
        return (col == wanted).astype(F32).astype(BF16)

    def order_back(e):
        col = lax.broadcasted_iota(jnp.int32, (all_rows, expert_rows), 1)
        at = lax.broadcasted_iota(jnp.int32, (all_rows, expert_rows), 0)
        wanted = (col // cap) * per_peer + e * cap + col % cap
        return (at == wanted).astype(F32).astype(BF16)

    def add_part(which, e, part):
        back = dot(order_back(e), part).reshape(n_ex, per_peer, width)
        x_send[which] = (x_send[which].astype(F32) + back).astype(BF16)

    def send_back(which):
        loop(1, n_ex, lambda i: y_copy(which, i).start())
        y_got[which, my_ex] = x_send[which, my_ex]

    def one_expert(e):
        c = 3 * e
        more = e < members - 1

        @pl.when(e == 0)
        def _():
            loop(1, n_ex, lambda i: x_copy(0, i).wait_recv())

        rows[...] = dot(order(e), x_got[0].reshape(all_rows, width)).astype(BF16)
        rows_t[pl.ds(0, in_blocks)] = turned(rows[...])
        gating = sigma(
            jnp.sum(rows[...].astype(F32) * router[e], axis=1, keepdims=True)
        )
        assemble(c, w_gate, in_blocks, hid_blocks)

        @pl.when(e == 0)
        def _():
            forward(2)
            loop(3, 3 * members, send_weights)

        @pl.when(e > 0)
        def _():
            pass_on(c - 2)

        pre_gate[...] = dot(rows[...], w_gate[...])
        assemble(c + 1, w_up, in_blocks, hid_blocks)
        pre_up[...] = dot(rows[...], w_up[...])
        gate = pre_gate[...]
        hidden[...] = (gate * sigma(gate) * pre_up[...]).astype(BF16)

        @pl.when(e == 0)
        def _():
            loop(1, n_ex, lambda i: x_copy(1, i).wait_recv())

            def sent(i):
                for which in range(2):
                    x_copy(which, i).wait_send()

            loop(1, n_ex, sent)
            x_send[...] = jnp.zeros(x_send.shape, BF16)

        grad_rows = dot(order(e), x_got[1].reshape(all_rows, width))
        scaled[...] = (gating * grad_rows).astype(BF16)
        hidden_t[pl.ds(0, hid_blocks)] = turned(hidden[...])
        scaled_t[...] = turned(scaled[...])
        assemble(c + 2, w_down, hid_blocks, in_blocks)
        extract(c + 2, hidden_t, scaled_t)
        pl.when(more)(lambda: forward(c + 3))
        pl.when(more)(lambda: forward(c + 4))
        hidden_grad = dot(scaled[...], w_down[...], ((1,), (1,)))
        pl.when(more)(lambda: forward(c + 5))
        gate = pre_gate[...]
        sig = sigma(gate)
        gate_grad = hidden_grad * pre_up[...] * sig * (1.0 + gate * (1.0 - sig))
        up_grad = hidden_grad * gate * sig
        pre_gate[...] = gate_grad
        pre_up[...] = up_grad
        inner_t[...] = turned(pre_gate[...].astype(BF16))
        extract(c, rows_t, inner_t)
        pass_on(c + 2)
        inner_t[...] = turned(pre_up[...].astype(BF16))
        extract(c + 1, rows_t, inner_t)
        pass_on(c)
        outs[...] = dot(hidden[...], w_down[...])
        add_part(0, e, (gating * outs[...]).astype(BF16))
        grad_rows = dot(order(e), x_got[1].reshape(all_rows, width))
        logit = (
            jnp.sum(grad_rows * outs[...], axis=1, keepdims=True) * gating * (1.0 - gating)
        )
        r_send[e] = jnp.sum(rows[...].astype(F32) * logit, axis=0, keepdims=True)

        @pl.when(e == members - 1)
        def _():
            for i in range(1, n_dp):
                r_copy(i).start()
            send_back(0)

        part = dot(pre_gate[...].astype(BF16), w_gate[...], ((1,), (1,)))
        part = part + dot(pre_up[...].astype(BF16), w_up[...], ((1,), (1,)))
        add_part(1, e, (part + logit * router[e]).astype(BF16))

    loop(0, members, one_expert)
    send_back(1)
    pass_on(3 * members - 2)

    def finish(c):
        for k in range(2, 6):
            g_copy(c, k).wait_recv()

        def add(q):
            total = own[c, q].astype(F32)
            for k in range(2):
                total = total + got[c, k, q].astype(F32)
            tiles[pl.ds(pl.multiple_of(q * BS, BS), BS), :] = total

        loop(0, pairs, add, 4)

        def separate(q):
            even = tiles[pl.ds(q * BS, half, stride=2), :]
            odd = tiles[pl.ds(q * BS + 1, half, stride=2), :]
            paired[pl.ds(pl.multiple_of(q * half, half), half), :] = jnp.where(
                half_low, even, pltpu.roll(odd, BS, 1)
            )
            paired[pl.ds(pl.multiple_of((q + pairs) * half, half), half), :] = jnp.where(
                half_low, pltpu.roll(even, BS, 1), odd
            )

        loop(0, pairs, separate, 8)
        score = jnp.zeros((2 * pairs, LANES), F32)
        for j in range(half):
            part = paired[pl.ds(j, 2 * pairs, stride=half), :]
            master = masters[c, :, j * LANES : (j + 1) * LANES]
            master_new[c, :, j * LANES : (j + 1) * LANES] = master - LEARN_RATE * part
            score = score + master * part
        score_sum[c] = jnp.sum(score, axis=1, keepdims=True)

    def finish_expert(e):
        for m in (2, 0, 1):
            finish(3 * e + m)

    loop(0, members - 1, finish_expert)
    placed = (
        lax.broadcasted_iota(jnp.int32, (tokens.shape[0], all_rows), 0) == picks_row[...]
    ).astype(F32).astype(BF16)
    loop(1, n_ex, lambda i: y_copy(0, i).wait_recv())
    layer_out[...] = dot(placed, y_got[0].reshape(all_rows, width)).astype(BF16)
    loop(1, n_ex, lambda i: y_copy(1, i).wait_recv())
    input_grad[...] = dot(placed, y_got[1].reshape(all_rows, width)).astype(BF16)

    for i in range(1, n_dp):
        r_copy(i).wait()
    share = width // n_dp
    mine = pl.ds(pl.multiple_of(my_dp * share, share), share)
    for e in range(members):
        router_total = r_send[e, :, mine]
        for i in range(1, n_dp):
            router_total = router_total + r_got[i - 1, e, :, mine]
        router_out[e] = router_total

    finish_expert(members - 1)

    def drain_weights(c):
        for k in range(6):
            g_copy(c, k).wait_send()

    loop(0, 3 * members, drain_weights)

    def drain_rows(i):
        for which in range(2):
            y_copy(which, i).wait_send()

    loop(1, n_ex, drain_rows)


def body(tokens, out_grad, token_picks, router, kept_blocks, masters, scores):
    members = kept_blocks.shape[0]
    slots = kept_blocks.shape[2]
    n_ex = lax.axis_size("expert")
    n_dp = lax.axis_size("dp")
    cap = token_picks.shape[2]
    width = tokens.shape[1]
    in_blocks = width // BS
    hid_blocks = FF // BS
    blocks = in_blocks * hid_blocks
    local = masters.shape[2]
    pairs = local // 2
    total_pairs = pairs * n_dp
    chunks = 3 * members
    all_rows = n_ex * members * cap
    expert_rows = n_ex * cap

    kept = kept_blocks.reshape(chunks, slots)
    numbers = jnp.arange(blocks, dtype=jnp.int32)
    hits = kept[:, None, :] == numbers[None, :, None]
    slot_of = jnp.sum(
        jnp.where(hits, jnp.arange(slots, dtype=jnp.int32) + 1, 0), axis=2
    ) - 1
    within = slot_of % local
    flipped = (within // pairs) != (numbers % 2)[None, :]
    place = (slot_of // local) * pairs + within % pairs + jnp.where(flipped, total_pairs, 0)
    place = jnp.where(slot_of >= 0, place, 2 * total_pairs).reshape(-1)

    col_counts = jnp.array([hid_blocks, hid_blocks, in_blocks] * members, jnp.int32)[:, None]
    empty = jnp.array([in_blocks, in_blocks, hid_blocks] * members, jnp.int32)[:, None] * BS
    code = (kept // col_counts) * BS + kept % col_counts
    code = jnp.where(kept < blocks, code, empty).reshape(-1)

    picks = token_picks[0].reshape(-1)
    router_rows = router.T.astype(F32).reshape(members, 1, width)

    vmem = pl.BlockSpec(memory_space=pltpu.VMEM)
    smem = pl.BlockSpec(memory_space=pltpu.SMEM)
    dma = pltpu.SemaphoreType.DMA
    layer_out, input_grad, master_new, score_sum, router_grad = pl.pallas_call(
        functools.partial(kernel, (n_dp, n_ex, members, cap)),
        out_shape=(
            jax.ShapeDtypeStruct(tokens.shape, BF16),
            jax.ShapeDtypeStruct(tokens.shape, BF16),
            jax.ShapeDtypeStruct((chunks, local, BS * BS), F32),
            jax.ShapeDtypeStruct((chunks, local, 1), F32),
            jax.ShapeDtypeStruct((members, 1, width // n_dp), F32),
        ),
        in_specs=[smem, smem] + [vmem] * 6,
        out_specs=[vmem] * 5,
        scratch_shapes=[
            pltpu.VMEM((chunks, pairs, BS, LANES), BF16),
            pltpu.VMEM((local * BS // 2, LANES), F32),
            pltpu.VMEM((pairs * BS, LANES), F32),
            pltpu.VMEM((chunks, n_dp - 1, pairs, BS, LANES), BF16),
            pltpu.VMEM((2 * total_pairs + 1, BS, LANES), BF16),
            pltpu.VMEM((width, FF), BF16),
            pltpu.VMEM((width, FF), BF16),
            pltpu.VMEM((FF, width), BF16),
            pltpu.VMEM((in_blocks + 1, BS, expert_rows), BF16),
            pltpu.VMEM((hid_blocks + 1, BS, expert_rows), BF16),
            pltpu.VMEM((in_blocks, BS, expert_rows), BF16),
            pltpu.VMEM((hid_blocks, BS, expert_rows), BF16),
            pltpu.VMEM((chunks, 2, pairs, BS, LANES), BF16),
            pltpu.VMEM((chunks, 2, pairs // 2, BS, LANES), BF16),
            pltpu.VMEM((2, n_ex, members * cap, width), BF16),
            pltpu.VMEM((2, n_ex, members * cap, width), BF16),
            pltpu.VMEM((2, n_ex, members * cap, width), BF16),
            pltpu.VMEM((expert_rows, width), BF16),
            pltpu.VMEM((expert_rows, width), BF16),
            pltpu.VMEM((expert_rows, FF), BF16),
            pltpu.VMEM((expert_rows, FF), F32),
            pltpu.VMEM((expert_rows, FF), F32),
            pltpu.VMEM((expert_rows, width), F32),
            pltpu.VMEM((members, 1, width), F32),
            pltpu.VMEM((n_dp - 1, members, 1, width), F32),
            dma((chunks, 4)),
            dma((chunks, 4)),
            dma((chunks, 6)),
            dma((chunks, 6)),
            dma((2, n_ex - 1)),
            dma((2, n_ex - 1)),
            dma((2, n_ex - 1)),
            dma((2, n_ex - 1)),
            dma((n_dp - 1,)),
            dma((n_dp - 1,)),
        ],
        compiler_params=pltpu.CompilerParams(
            collective_id=0, has_side_effects=True, vmem_limit_bytes=62 * 1024 * 1024
        ),
    )(
        place,
        code,
        picks.reshape(all_rows, 1),
        picks.reshape(1, all_rows),
        tokens,
        out_grad,
        router_rows,
        masters.reshape(chunks, local, BS * BS),
    )

    master_new = master_new.reshape(masters.shape)
    score_new = scores - SCORE_RATE * score_sum.reshape(scores.shape)
    return layer_out, input_grad, master_new, score_new, router_grad.reshape(members, -1).T


def solution(mesh):
    return jax.shard_map(
        body,
        mesh=mesh,
        in_specs=(
            P(("dp", "expert"), None),
            P(("dp", "expert"), None),
            P(("dp", "expert"), None, None),
            P(None, "expert"),
            P("expert", None, None),
            P("expert", None, "dp", None),
            P("expert", None, "dp"),
        ),
        out_specs=(
            P(("dp", "expert"), None),
            P(("dp", "expert"), None),
            P("expert", None, "dp", None),
            P("expert", None, "dp"),
            P("dp", "expert"),
        ),
        check_vma=False,
    )
```
